256 devices in a mesh: row: 32 (over z_lo, y, core), col: 8 (over x, z_hi).
Axes of the slice: x: 4, y: 4, z: 8 (z_hi: 2, z_lo: 4; z = z_hi * 4 + z_lo), core: 2. Of those that a mesh axis runs over, the one named last changes fastest.
Arguments:
- queries: bfloat16 [32768, 128], P(('col', 'row')), may hold values from -4 to 4
- keys: bfloat16 [61440, 128], P(('row', 'col')), may hold values from -4 to 4
- values: bfloat16 [61440, 128], P(('row', 'col')), may hold values from -6 to 6
- outputs: bfloat16 [32768, 128], P(('col', 'row')), may hold values from -6 to 6
- out_grad: bfloat16 [32768, 128], P(('col', 'row')), may hold values from -96 to 96
- lse: float32 [32768], P(('col', 'row')), as said below
Outputs:
- grad_queries: float32 [32768, 128], P(('col', 'row'))
- grad_keys: float32 [61440, 128], P(('row', 'col'))
- grad_values: float32 [61440, 128], P(('row', 'col'))
The draws below stay inside these ranges and needn't reach their ends.
Inputs may be any that keep to these rules, and one draw needn't show every extreme that they name: `lse`: each value is the natural logarithm of 61440 plus a number between 0.05 and 0.9.
All inputs are finite; a program needn't handle non-finite values.
Results may differ from the reference program's by a relative error of at most 0.0029.
Values may be sent and summed in bfloat16 or wider, within the bound.
No kernel may reach another device: no remote copies, remote signals or barrier semaphores. Data moves between devices by JAX's collectives and lax.ppermute only.
A program may use at most 64 MiB of HBM per device.

```python
import math
import jax
import jax.numpy as jnp
from jax import lax

HD = 128
NQ = 32768
NK = 61440


def clipped_normal(key, count):
    base = jax.random.normal(key, (count, HD), jnp.float32)
    return jnp.clip(base, -4.0, 4.0).astype(jnp.bfloat16)


def draw_queries(key, part):
    key = jax.random.fold_in(key, 11)
    return clipped_normal(key, NQ)


def draw_keys(key, part):
    key = jax.random.fold_in(key, 13)
    return clipped_normal(key, NK)


def draw_lse(key, part):
    key = jax.random.fold_in(key, 7)
    centre = math.log(NK) + 0.5
    jitter = jax.random.uniform(key, (NQ,), jnp.float32, -0.4, 0.4)
    return centre + jitter


def level_of(rng, shape, cuts, low, top_value):
    factor_of, own = 1.0, jax.random.fold_in(rng, 6)
    for position, blocks in cuts:
        heights = jnp.exp(jax.random.uniform(jax.random.fold_in(own, position), (blocks,), jnp.float32, low / len(cuts), top_value / len(cuts)))
        factor_of = factor_of * jnp.repeat(heights, shape[position] // blocks).reshape([-1 if axis == position else 1 for axis in range(len(shape))])
    return factor_of


def scatter_about(key, dims, width, reach, cuts=(), held_as=jnp.bfloat16):
    loudness = level_of(key, dims, cuts, -0.22, 0.18) if cuts else 1.0
    drawn = jax.random.normal(key, dims, jnp.float32) * width * loudness
    return jnp.minimum(jnp.maximum(drawn, -reach), reach).astype(held_as)


def setup_inputs(seed: int = 0) -> dict:
    key_of = jax.random.split(jax.random.key(seed), 7)
    return {
        "queries": draw_queries(jax.random.fold_in(key_of[6], 71), 0),
        "keys": draw_keys(jax.random.fold_in(key_of[6], 71), 0),
        "values": scatter_about(key_of[2], (NK, HD), 1.0, 6.0, ((0, 256),)),
        "outputs": scatter_about(key_of[3], (NQ, HD), 1.0, 6.0, ((0, 256),)),
        "out_grad": scatter_about(key_of[4], (NQ, HD), 16.0, 96.0, ((0, 256),)),
        "lse": draw_lse(jax.random.fold_in(key_of[6], 71), 0),
    }


def reference(queries, keys, values, outputs, out_grad, lse):
    factor = 1.0 / math.sqrt(HD)
    delta = lax.optimization_barrier(jnp.sum(out_grad.astype(jnp.float32) * outputs.astype(jnp.float32), axis=1))
    count = queries.shape[0]
    block = 512 if count % 512 == 0 else count
    nblocks = count // block
    q_blocks = queries.reshape(nblocks, block, HD)
    g_blocks = out_grad.reshape(nblocks, block, HD)
    l_blocks = lse.reshape(nblocks, block)
    d_blocks = delta.reshape(nblocks, block)

    def step(carry, pieces):
        grad_k, grad_v = carry
        q_rows, g_rows, l_rows, d_rows = pieces
        scores = jnp.dot(q_rows, keys.T, preferred_element_type=jnp.float32) * factor
        probs = jnp.exp(scores - l_rows[:, None])
        probs_low = probs.astype(jnp.bfloat16)
        grad_v = grad_v + jnp.dot(probs_low.T, g_rows, preferred_element_type=jnp.float32)
        dprobs = jnp.dot(g_rows, values.T, preferred_element_type=jnp.float32)
        dscores = (probs * (dprobs - d_rows[:, None])).astype(jnp.bfloat16)
        grad_q = jnp.dot(dscores, keys, preferred_element_type=jnp.float32) * factor
        grad_k = grad_k + jnp.dot(dscores.T, q_rows, preferred_element_type=jnp.float32) * factor
        return ((grad_k, grad_v), grad_q)
    zeros = jnp.zeros(keys.shape, jnp.float32)
    (grad_k, grad_v), grad_q = lax.scan(step, (zeros, zeros), (q_blocks, g_blocks, l_blocks, d_blocks))
    return (grad_q.reshape(count, HD), grad_k, grad_v)
```

```python
import math

import jax
import jax.numpy as jnp
from jax import lax
from jax.experimental import pallas as pl
from jax.experimental.pallas import tpu as pltpu
from jax.sharding import Mesh, PartitionSpec as P

W = 128
KA, KB = 128, 112
QP = 2 * W + 16
BF, F32 = jnp.bfloat16, jnp.float32
FACTOR = 1.0 / math.sqrt(W)
LOG2E = math.log2(math.e)
NT = (((1,), (1,)), ((), ()))
NN = (((1,), (0,)), ((), ()))
TN = (((0,), (0,)), ((), ()))
VM = pl.BlockSpec(memory_space=pltpu.VMEM)


def dot(a, b, dims):
    return lax.dot_general(a, b, dims, preferred_element_type=F32)


def call(kernel, name, outs, args, flops=0, aliases=None):
    nbytes = sum(math.prod(a.shape) * a.dtype.itemsize for a in list(outs) + list(args))
    return pl.pallas_call(
        kernel,
        name=name,
        out_shape=outs,
        in_specs=[VM] * len(args),
        out_specs=tuple([VM] * len(outs)),
        input_output_aliases=aliases or {},
        compiler_params=pltpu.CompilerParams(vmem_limit_bytes=40 * 2**20),
        cost_estimate=pl.CostEstimate(flops=flops, bytes_accessed=nbytes, transcendentals=0),
    )(*args)


def sds(shape, dtype):
    return jax.ShapeDtypeStruct(shape, dtype)


def pack_kernel(q, g, o, lse, k, v, qp, a, b):
    qp[0:W, :] = q[...]
    qp[W : 2 * W, :] = g[...]
    prod = g[...].astype(F32) * o[...].astype(F32)
    delta = jnp.sum(prod.T, axis=0, keepdims=True)
    rows = []
    for x in (lse[...] * LOG2E, delta):
        for _ in range(3):
            part = x.astype(BF).astype(F32)
            rows.append(part)
            x = x - part
    rows.append(jnp.zeros((10, W), F32))
    qp[2 * W :, :] = jnp.concatenate(rows, axis=0).astype(BF)
    a[0:KA, :] = k[0:KA, :]
    a[KA : 2 * KA, :] = v[0:KA, :]
    b[0:KB, :] = k[KA:, :]
    b[KB : 2 * KB, :] = v[KA:, :]


def chunk_kernel(first, chip, mine, sib, ka, kb, *rest):
    if first:
        oa, ob, gc, gm, gs = rest
        acc_in = None
    else:
        acc_in, (oa, ob, gc, gm, gs) = rest[:3], rest[3:]
    shards = [(0, i) for i in range(2)] + [(1, i) for i in range(7)] + [(2, i) for i in range(7)]
    qrefs, accs = (chip, mine, sib), (gc, gm, gs)
    ks = jnp.concatenate([ka[i, 0:KA, :] for i in range(4)] + [kb[i, 0:KB, :] for i in range(4)], axis=0)
    vs = jnp.concatenate([ka[i, KA:, :] for i in range(4)] + [kb[i, KB:, :] for i in range(4)], axis=0)
    gk = gv = None
    for j in range(4):
        mem = shards[4 * j : 4 * j + 4]
        q = jnp.concatenate([qrefs[r][i, 0:W, :] for r, i in mem], axis=0)
        g = jnp.concatenate([qrefs[r][i, W : 2 * W, :] for r, i in mem], axis=0)
        stat = jnp.concatenate([qrefs[r][i, 2 * W :, :].astype(F32) for r, i in mem], axis=1)
        l2 = stat[0:1] + stat[1:2] + stat[2:3]
        delta = stat[3:4] + stat[4:5] + stat[5:6]
        p = jnp.exp2(dot(ks, q, NT) * (FACTOR * LOG2E) - l2)
        ds = (p * (dot(vs, g, NT) - delta)).astype(BF)
        dv = dot(p.astype(BF), g, NN)
        dk = dot(ds, q, NN)
        gv = dv if gv is None else gv + dv
        gk = dk if gk is None else gk + dk
        u = dot(ks, ds, TN)
        for n, (r, i) in enumerate(mem):
            part = u[:, n * W : (n + 1) * W]
            accs[r][i] = part if first else acc_in[r][i] + part
    for i in range(4):
        rows = slice(i * KA, (i + 1) * KA)
        oa[i, 0:KA, :] = gk[rows].astype(oa.dtype)
        oa[i, KA:, :] = gv[rows].astype(oa.dtype)
        rows = slice(4 * KA + i * KB, 4 * KA + (i + 1) * KB)
        ob[i, 0:KB, :] = gk[rows].astype(ob.dtype)
        ob[i, KB:, :] = gv[rows].astype(ob.dtype)


def chunk(name, chip, mine, sib, ka, kb, acc, dtype):
    outs = (
        sds((4, 2 * KA, W), dtype),
        sds((4, 2 * KB, W), dtype),
        sds((2, W, W), F32),
        sds((7, W, W), F32),
        sds((7, W, W), F32),
    )
    args = (chip, mine, sib, ka, kb)
    aliases = {}
    if acc is not None:
        args += acc
        aliases = {5: 2, 6: 3, 7: 4}

    def kernel(*refs):
        chunk_kernel(acc is None, *refs)

    out = call(kernel, name, outs, args, flops=10 * 960 * 2048 * W, aliases=aliases)
    return out[0], out[1], tuple(out[2:])


def merge_kernel(a0, a1, a2, a3, b0, b1, b2, b3, *outs):
    for own, others, out in ((a0, (a1, a2, a3), outs[:4]), (b0, (b1, b2, b3), outs[4:])):
        for r in range(4):
            total = own[r]
            for other in others:
                total = total + other[r].astype(F32)
            out[r][...] = total.astype(out[r].dtype)


def keys_kernel(a0, a1, a2, a3, b0, b1, b2, b3, gk, gv):
    ta = a0[...] + a1[...].astype(F32) + a2[...].astype(F32) + a3[...].astype(F32)
    tb = b0[...] + b1[...].astype(F32) + b2[...].astype(F32) + b3[...].astype(F32)
    gk[0:KA, :] = ta[0:KA] * FACTOR
    gv[0:KA, :] = ta[KA:]
    gk[KA:, :] = tb[0:KB] * FACTOR
    gv[KA:, :] = tb[KB:]


def halves_kernel(gm, rs, m1, m2, m3, m4):
    for n, out in enumerate((m1, m2, m3)):
        out[...] = (gm[2 * n : 2 * n + 2] + rs[2 * n : 2 * n + 2]).astype(BF)
    m4[...] = (gm[6:7] + rs[6:7]).astype(BF)


def rows_kernel(gc, u1, u2, u3, u4, own, other):
    total = gc[...] + u1[...].astype(F32) + u2[...].astype(F32) + u3[...].astype(F32)
    own[...] = total[0] + u4[0].astype(F32)
    other[...] = total[1]


def queries_kernel(own, got, gq):
    gq[...] = (own[...] + got[...]).T * FACTOR


def shift4(s):
    return [(i, (i + s) % 4) for i in range(4)]


SWAP = [(0, 1), (1, 0)]


def along_z(s):
    index = lambda z, c: (z % 4) * 4 + c * 2 + z // 4
    return [
        (index(z, c), index((z + (s if c == 0 else -s)) % 8, c)) for z in range(8) for c in range(2)
    ]


def send_z(x, s):
    return lax.ppermute(x, ("zl", "core", "zh"), along_z(s))


def local(queries, keys, values, outputs, out_grad, lse):
    qp, a, b = call(
        pack_kernel,
        "pack",
        (sds((QP, W), BF), sds((2 * KA, W), BF), sds((2 * KB, W), BF)),
        (queries, out_grad, outputs, lse.reshape(1, W), keys, values),
    )
    qx = lax.ppermute(qp, "core", SWAP)
    chip = jnp.stack([qp, qx])
    ka = jnp.stack([a] + [lax.ppermute(a, "x", shift4(r)) for r in (1, 2, 3)])
    kb = jnp.stack([b] + [lax.ppermute(b, "y", shift4(r)) for r in (1, 2, 3)])
    q4 = send_z(qp, 4)
    mine = jnp.concatenate([send_z(chip, s) for s in (1, 2, 3)] + [q4[None]])
    sib = lax.ppermute(mine, "core", SWAP)

    acc = None
    back_a, back_b = {}, {}
    for s in (1, 3, 2):
        ka_s = lax.ppermute(ka, "y", shift4(s))
        kb_s = lax.ppermute(kb, "x", shift4(s))
        oa, ob, acc = chunk(f"chunk{s}", chip, mine, sib, ka_s, kb_s, acc, BF)
        back_a[s] = lax.ppermute(oa, "y", shift4(-s))
        back_b[s] = lax.ppermute(ob, "x", shift4(-s))
    oa, ob, (gc, gm, gs) = chunk("chunk0", chip, mine, sib, ka, kb, acc, F32)

    rs = lax.ppermute(gs, "core", SWAP)
    m1, m2, m3, m4 = call(
        halves_kernel, "halves", (sds((2, W, W), BF),) * 3 + (sds((1, W, W), BF),), (gm, rs)
    )
    u1, u2, u3 = (send_z(m, -s) for s, m in ((1, m1), (2, m2), (3, m3)))
    u4 = send_z(m4, 4)

    merged = call(
        merge_kernel,
        "merge",
        (sds((2 * KA, W), F32),) + (sds((2 * KA, W), BF),) * 3 + (sds((2 * KB, W), F32),) + (sds((2 * KB, W), BF),) * 3,
        (oa, *(back_a[s] for s in (1, 2, 3)), ob, *(back_b[s] for s in (1, 2, 3))),
    )
    fa = [lax.ppermute(merged[r], "x", shift4(-r)) for r in (1, 2, 3)]
    fb = [lax.ppermute(merged[4 + r], "y", shift4(-r)) for r in (1, 2, 3)]

    own, other = call(rows_kernel, "rows", (sds((W, W), F32),) * 2, (gc, u1, u2, u3, u4))
    got = lax.ppermute(other, "core", SWAP)
    gk, gv = call(keys_kernel, "keys", (sds((KA + KB, W), F32),) * 2, (merged[0], *fa, merged[4], *fb))
    (gq,) = call(queries_kernel, "queries", (sds((W, W), F32),), (own, got))
    return gq, gk, gv


def solution(mesh):
    fine = Mesh(mesh.devices.reshape(4, 4, 2, 4, 2), ("zl", "y", "core", "x", "zh"))
    qs, ks = ("x", "zh", "zl", "y", "core"), ("zl", "y", "core", "x", "zh")
    return jax.shard_map(
        local,
        mesh=fine,
        in_specs=(P(qs, None), P(ks, None), P(ks, None), P(qs, None), P(qs, None), P(qs)),
        out_specs=(P(qs, None), P(ks, None), P(ks, None)),
        check_vma=False,
    )
```

```python
import math

import jax
import jax.numpy as jnp
from jax import lax
from jax.experimental import pallas as pl
from jax.experimental.pallas import tpu as pltpu
from jax.sharding import Mesh, PartitionSpec as P

W = 128
T = 240
QP = 2 * W + 16
BF, F32 = jnp.bfloat16, jnp.float32
FACTOR = 1.0 / math.sqrt(W)
LOG2E = math.log2(math.e)
NT = (((1,), (1,)), ((), ()))
NN = (((1,), (0,)), ((), ()))
TN = (((0,), (0,)), ((), ()))
VM = pl.BlockSpec(memory_space=pltpu.VMEM)
ANY = pl.BlockSpec(memory_space=pl.ANY)


def dot(a, b, dims):
    return lax.dot_general(a, b, dims, preferred_element_type=F32)


def call(kernel, name, outs, args, flops=0, aliases=None, spaces=None, scratch=(), vmem=40):
    nbytes = sum(math.prod(a.shape) * a.dtype.itemsize for a in list(outs) + list(args))
    return pl.pallas_call(
        kernel,
        name=name,
        out_shape=outs,
        in_specs=spaces or [VM] * len(args),
        out_specs=tuple([VM] * len(outs)),
        input_output_aliases=aliases or {},
        scratch_shapes=list(scratch),
        compiler_params=pltpu.CompilerParams(vmem_limit_bytes=vmem * 2**20),
        cost_estimate=pl.CostEstimate(flops=flops, bytes_accessed=nbytes, transcendentals=0),
    )(*args)


def sds(shape, dtype):
    return jax.ShapeDtypeStruct(shape, dtype)


def pack_kernel(q, g, o, lse, k, v, qp, kv, obuf, lbuf, sems):
    copies = [
        pltpu.make_async_copy(src, dst, sems.at[n])
        for n, (src, dst) in enumerate(
            (
                (g, qp.at[pl.ds(W, W), :]),
                (o, obuf),
                (lse, lbuf),
                (q, qp.at[pl.ds(0, W), :]),
                (k, kv.at[pl.ds(0, T), :]),
                (v, kv.at[pl.ds(T, T), :]),
            )
        )
    ]
    for copy in copies:
        copy.start()
    for copy in copies:
        copy.wait()
    prod = qp[W : 2 * W, :].astype(F32) * obuf[...].astype(F32)
    delta = jnp.sum(prod.T, axis=0, keepdims=True)
    rows = []
    for x in (lbuf[...] * LOG2E, delta):
        for _ in range(3):
            part = x.astype(BF).astype(F32)
            rows.append(part)
            x = x - part
    rows.append(jnp.zeros((10, W), F32))
    qp[2 * W :, :] = jnp.concatenate(rows, axis=0).astype(BF)


SHARDS = (
    [(0, i) for i in range(4)],
    [(1, i) for i in range(4)],
    [(2, i) for i in range(4)],
    [(1, 4), (1, 5), (2, 4), (2, 5)],
)


def chunk_kernel(first, chip, mine, sib, kv, *rest):
    if first:
        out, gc, gm, gs = rest
        acc_in = None
    else:
        acc_in, (out, gc, gm, gs) = rest[:3], rest[-4:]
    qrefs, accs = (chip, mine, sib), (gc, gm, gs)
    ks = jnp.concatenate([kv[i, 0:T, :] for i in range(4)], axis=0)
    vs = jnp.concatenate([kv[i, T:, :] for i in range(4)], axis=0)
    gk = gv = None
    for mem in SHARDS:
        q = jnp.concatenate([qrefs[r][i, 0:W, :] for r, i in mem], axis=0)
        g = jnp.concatenate([qrefs[r][i, W : 2 * W, :] for r, i in mem], axis=0)
        stat = jnp.concatenate([qrefs[r][i, 2 * W :, :].astype(F32) for r, i in mem], axis=1)
        l2 = stat[0:1] + stat[1:2] + stat[2:3]
        delta = stat[3:4] + stat[4:5] + stat[5:6]
        p = jnp.exp2(dot(ks, q, NT) * (FACTOR * LOG2E) - l2)
        ds = (p * (dot(vs, g, NT) - delta)).astype(BF)
        dv = dot(p.astype(BF), g, NN)
        dk = dot(ds, q, NN)
        gv = dv if gv is None else gv + dv
        gk = dk if gk is None else gk + dk
        u = dot(ks, ds, TN)
        for n, (r, i) in enumerate(mem):
            part = u[:, n * W : (n + 1) * W]
            accs[r][i] = part if first else acc_in[r][i] + part
    for i in range(4):
        rows = slice(i * T, (i + 1) * T)
        out[i, 0:T, :] = gk[rows].astype(out.dtype)
        out[i, T:, :] = gv[rows].astype(out.dtype)


def chunk(name, chip, mine, sib, kv, acc, dtype, after=()):
    outs = (sds((4, 2 * T, W), dtype), sds((4, W, W), F32), sds((6, W, W), F32), sds((6, W, W), F32))
    args = (chip, mine, sib, kv)
    aliases = {}
    if acc is not None:
        args += acc
        aliases = {4: 1, 5: 2, 6: 3}
    spaces = [VM] * len(args) + [ANY] * len(after)

    def kernel(*refs):
        chunk_kernel(acc is None, *refs)

    out = call(kernel, name, outs, args + tuple(after), 10 * 960 * 2048 * W, aliases, spaces)
    return out[0], tuple(out[1:])


def merge_kernel(own, b1, b2, b3, *outs):
    for r in range(4):
        total = own[r]
        for other in (b1, b2, b3):
            total = total + other[r].astype(F32)
        outs[r][...] = total.astype(outs[r].dtype)


def halves_kernel(gm, rs, after, m1, m2):
    m1[...] = (gm[0:4] + rs[0:4]).astype(BF)
    m2[...] = (gm[4:6] + rs[4:6]).astype(BF)


def rows_kernel(gc, u1, u2, own, other):
    own[...] = gc[0:2] + u1[0:2].astype(F32) + u2[...].astype(F32)
    other[...] = gc[2:4] + u1[2:4].astype(F32)


def pair_kernel(own, got, near, far):
    near[...] = own[0] + got[0]
    far[...] = own[1] + got[1]


def last_kernel(near, far, own, f1, f2, f3, gq, gk, gv):
    gq[...] = (near[...] + far[...]).T * FACTOR
    total = own[...] + f1[...].astype(F32) + f2[...].astype(F32) + f3[...].astype(F32)
    gk[...] = total[0:T] * FACTOR
    gv[...] = total[T:]


SWAP = [(0, 1), (1, 0)]
FAR = [(0, 1), (1, 0)]


def swap_cores(x):
    return lax.ppermute(x, "core", SWAP)


def swap_halves(x):
    return lax.ppermute(x, "zh", FAR)


def send_z(x, s):
    index = lambda z, c: (z % 4) * 4 + c * 2 + z // 4
    pairs = [
        (index(z, c), index((z + (s if c == 0 else -s)) % 8, c)) for z in range(8) for c in range(2)
    ]
    return lax.ppermute(x, ("zl", "core", "zh"), pairs)


def send_plane(x, s, core_on_x):
    pairs = []
    for y in range(4):
        for c in range(2):
            for i in range(4):
                to_y, to_x = (y, (i + s) % 4) if c == core_on_x else ((y + s) % 4, i)
                pairs.append(((y * 2 + c) * 4 + i, (to_y * 2 + c) * 4 + to_x))
    return lax.ppermute(x, ("y", "core", "x"), pairs)


def local(queries, keys, values, outputs, out_grad, lse):
    qp, kv = call(
        pack_kernel,
        "pack",
        (sds((QP, W), BF), sds((2 * T, W), BF)),
        (queries, out_grad, outputs, lse.reshape(1, W), keys, values),
        spaces=[ANY] * 6,
        scratch=(pltpu.VMEM((W, W), BF), pltpu.VMEM((1, W), F32), pltpu.SemaphoreType.DMA((6,))),
        vmem=60,
    )
    pair = jnp.stack([qp, swap_halves(qp)])
    chip = jnp.concatenate([pair, swap_cores(pair)])
    mine = jnp.concatenate([send_z(chip, 1), send_z(pair, 2)])
    sib = swap_cores(mine)
    kv0 = jnp.stack([kv] + [send_plane(kv, r, 0) for r in (1, 2, 3)])
    kvs = {s: send_plane(kv0, s, 1) for s in (1, 3, 2)}

    out1, acc = chunk("chunk1", chip, mine, sib, kvs[1], None, BF)
    back1 = send_plane(out1, -1, 1)
    out3, acc = chunk("chunk3", chip, mine, sib, kvs[3], acc, BF)
    back3 = send_plane(out3, -3, 1)
    out2, acc = chunk("chunk2", chip, mine, sib, kvs[2], acc, BF, (back1,))
    back2 = send_plane(out2, -2, 1)
    out0, (gc, gm, gs) = chunk("chunk0", chip, mine, sib, kv0, acc, F32, (back3,))

    rs = swap_cores(gs)
    part0, *parts = call(
        merge_kernel,
        "merge",
        (sds((2 * T, W), F32),) + (sds((2 * T, W), BF),) * 3,
        (out0, back1, back2, back3),
    )
    f1, f2, f3 = (send_plane(parts[r - 1], -r, 0) for r in (1, 2, 3))
    m1, m2 = call(
        halves_kernel,
        "halves",
        (sds((4, W, W), BF), sds((2, W, W), BF)),
        (gm, rs, part0),
        spaces=[VM, VM, ANY],
    )
    u1, u2 = send_z(m1, -1), send_z(m2, -2)
    own, other = call(rows_kernel, "rows", (sds((2, W, W), F32),) * 2, (gc, u1, u2))
    near, far = call(pair_kernel, "pair", (sds((W, W), F32),) * 2, (own, swap_cores(other)))
    return call(
        last_kernel,
        "last",
        (sds((W, W), F32), sds((T, W), F32), sds((T, W), F32)),
        (near, swap_halves(far), part0, f1, f2, f3),
    )


def solution(mesh):
    fine = Mesh(mesh.devices.reshape(4, 4, 2, 4, 2), ("zl", "y", "core", "x", "zh"))
    qs, ks = ("x", "zh", "zl", "y", "core"), ("zl", "y", "core", "x", "zh")
    return jax.shard_map(
        local,
        mesh=fine,
        in_specs=(P(qs, None), P(ks, None), P(ks, None), P(qs, None), P(qs, None), P(qs)),
        out_specs=(P(qs, None), P(ks, None), P(ks, None)),
        check_vma=False,
    )
```

```python
import math

import jax
import jax.numpy as jnp
from jax import lax
from jax.experimental import pallas as pl
from jax.experimental.pallas import tpu as pltpu
from jax.sharding import Mesh, PartitionSpec as P

W = 128
T = 240
QP = 2 * W + 16
BF, F32 = jnp.bfloat16, jnp.float32
FACTOR = 1.0 / math.sqrt(W)
LOG2E = math.log2(math.e)
NT = (((1,), (1,)), ((), ()))
NN = (((1,), (0,)), ((), ()))
TN = (((0,), (0,)), ((), ()))
VM = pl.BlockSpec(memory_space=pltpu.VMEM)
ANY = pl.BlockSpec(memory_space=pl.ANY)


def dot(a, b, dims):
    return lax.dot_general(a, b, dims, preferred_element_type=F32)


def call(kernel, name, outs, args, flops=0, aliases=None, spaces=None, scratch=(), vmem=40):
    nbytes = sum(math.prod(a.shape) * a.dtype.itemsize for a in list(outs) + list(args))
    return pl.pallas_call(
        kernel,
        name=name,
        out_shape=outs,
        in_specs=spaces or [VM] * len(args),
        out_specs=tuple([VM] * len(outs)),
        input_output_aliases=aliases or {},
        scratch_shapes=list(scratch),
        compiler_params=pltpu.CompilerParams(vmem_limit_bytes=vmem * 2**20),
        cost_estimate=pl.CostEstimate(flops=flops, bytes_accessed=nbytes, transcendentals=0),
    )(*args)


def sds(shape, dtype):
    return jax.ShapeDtypeStruct(shape, dtype)


def pack_kernel(q, g, o, lse, k, v, qp, kv, qbuf, gbuf, obuf, lbuf, sems):
    moves = (
        (g, gbuf),
        (o, obuf),
        (lse, lbuf),
        (q, qbuf),
        (k, kv.at[pl.ds(0, T), :]),
        (v, kv.at[pl.ds(T, T), :]),
    )
    copies = [pltpu.make_async_copy(src, dst, sems.at[n]) for n, (src, dst) in enumerate(moves)]
    for copy in copies:
        copy.start()
    for copy in copies[:3]:
        copy.wait()
    prod = gbuf[...].astype(F32) * obuf[...].astype(F32)
    delta = jnp.sum(prod.T, axis=0, keepdims=True)
    rows = []
    for x in (lbuf[...] * LOG2E, delta):
        for _ in range(3):
            part = x.astype(BF).astype(F32)
            rows.append(part)
            x = x - part
    rows.append(jnp.zeros((10, W), F32))
    stat = jnp.concatenate(rows, axis=0).astype(BF)
    for copy in copies[3:]:
        copy.wait()
    for z in range(8):
        qp[z, 0:W, :] = qbuf[...]
        qp[z, W : 2 * W, :] = gbuf[...]
        qp[z, 2 * W :, :] = stat


SAME, OTHER = ((0, 0), (0, 4)), ((1, 0), (1, 4))


def chunk_kernel(groups, given, touched, has_part, refs):
    qrefs, kv, refs = refs[:2], refs[2], refs[3:]
    acc_in, refs = dict(zip(given, refs)), refs[len(given) :]
    part = refs[0] if has_part else None
    refs = refs[len(refs) - 1 - len(touched) :]
    out, accs = refs[0], dict(zip(touched, refs[1:]))
    ks = jnp.concatenate([kv[i, 0:T, :] for i in range(4)], axis=0)
    vs = jnp.concatenate([kv[i, T:, :] for i in range(4)], axis=0)
    gk = gv = None
    for r, at in groups:
        mem = range(at, at + 4)
        q = jnp.concatenate([qrefs[r][i, 0:W, :] for i in mem], axis=0)
        g = jnp.concatenate([qrefs[r][i, W : 2 * W, :] for i in mem], axis=0)
        stat = jnp.concatenate([qrefs[r][i, 2 * W :, :].astype(F32) for i in mem], axis=1)
        l2 = stat[0:1] + stat[1:2] + stat[2:3]
        delta = stat[3:4] + stat[4:5] + stat[5:6]
        p = jnp.exp2(dot(ks, q, NT) * (FACTOR * LOG2E) - l2)
        ds = (p * (dot(vs, g, NT) - delta)).astype(BF)
        dv = dot(p.astype(BF), g, NN)
        dk = dot(ds, q, NN)
        gv = dv if gv is None else gv + dv
        gk = dk if gk is None else gk + dk
        u = dot(ks, ds, TN)
        for n, i in enumerate(mem):
            block = u[:, n * W : (n + 1) * W]
            accs[r][i] = acc_in[r][i] + block if r in acc_in else block
    for i in range(4):
        rows = slice(i * T, (i + 1) * T)
        for col, total in ((slice(0, T), gk), (slice(T, 2 * T), gv)):
            block = total[rows]
            if has_part:
                block = part[i, col, :] + block
            out[i, col, :] = block.astype(out.dtype)


def chunk(name, queries, kv, acc, dtype, groups=SAME + OTHER, part=None, after=()):
    touched = sorted({r for r, _ in groups})
    given = [r for r in touched if r in acc]
    outs = (sds((4, 2 * T, W), dtype),) + (sds((8, W, W), F32),) * len(touched)
    args = tuple(queries) + (kv,)
    aliases = {len(args) + n: 1 + touched.index(r) for n, r in enumerate(given)}
    args += tuple(acc[r] for r in given)
    if part is not None:
        aliases[len(args)] = 0
        args += (part,)
    spaces = [VM] * len(args) + [ANY] * len(after)

    def kernel(*refs):
        chunk_kernel(groups, given, touched, part is not None, refs)

    flops = 10 * 960 * 512 * len(groups) * W
    out = call(kernel, name, outs, args + tuple(after), flops, aliases, spaces)
    return out[0], {**acc, **dict(zip(touched, out[1:]))}


def merge_kernel(own, b1, b2, b3, after, *outs):
    for r in range(4):
        total = own[r]
        for other in (b1, b2, b3):
            total = total + other[r].astype(F32)
        outs[r][...] = total.astype(outs[r].dtype)


def halves_kernel(mine, got, out):
    out[...] = (mine[...] + got[...]).astype(BF)


def last_kernel(u, own, f1, f2, f3, gq, gk, gv):
    total = u[0].astype(F32)
    for z in range(1, 8):
        total = total + u[z].astype(F32)
    gq[...] = total.T * FACTOR
    total = own[...] + f1[...].astype(F32) + f2[...].astype(F32) + f3[...].astype(F32)
    gk[...] = total[0:T] * FACTOR
    gv[...] = total[T:]


SWAP = [(0, 1), (1, 0)]


def swap_cores(x):
    return lax.ppermute(x, "core", SWAP)


def exchange_z(x):
    return lax.all_to_all(x, ("zl", "zh"), 0, 0, tiled=True)


def send_plane(x, s, core_on_x):
    pairs = []
    for y in range(4):
        for c in range(2):
            for i in range(4):
                to_y, to_x = (y, (i + s) % 4) if c == core_on_x else ((y + s) % 4, i)
                pairs.append(((y * 2 + c) * 4 + i, (to_y * 2 + c) * 4 + to_x))
    return lax.ppermute(x, ("y", "core", "x"), pairs)


def local(queries, keys, values, outputs, out_grad, lse):
    qp, kv = call(
        pack_kernel,
        "pack",
        (sds((8, QP, W), BF), sds((2 * T, W), BF)),
        (queries, out_grad, outputs, lse.reshape(1, W), keys, values),
        spaces=[ANY] * 6,
        scratch=(
            pltpu.VMEM((W, W), BF),
            pltpu.VMEM((W, W), BF),
            pltpu.VMEM((W, W), BF),
            pltpu.VMEM((1, W), F32),
            pltpu.SemaphoreType.DMA((6,)),
        ),
        vmem=60,
    )
    same = exchange_z(qp)
    other = swap_cores(same)
    kv0 = jnp.stack([kv] + [send_plane(kv, r, 0) for r in (1, 2, 3)])
    kvs = {s: send_plane(kv0, s, 1) for s in (1, 3, 2)}

    qs = (same, other)
    part, acc = chunk("chunk0a", qs, kv0, {}, F32, OTHER)
    out1, acc = chunk("chunk1", qs, kvs[1], acc, BF)
    back1 = send_plane(out1, -1, 1)
    out3, acc = chunk("chunk3", qs, kvs[3], acc, BF)
    back3 = send_plane(out3, -3, 1)
    out2, acc = chunk("chunk2", qs, kvs[2], acc, BF, after=(back1,))
    back2 = send_plane(out2, -2, 1)
    rs = swap_cores(acc[1])
    out0, acc = chunk("chunk0b", qs, kv0, acc, F32, SAME, part, (back3,))

    (halves,) = call(halves_kernel, "halves", (sds((8, W, W), BF),), (acc[0], rs))
    u = exchange_z(halves)
    part0, *parts = call(
        merge_kernel,
        "merge",
        (sds((2 * T, W), F32),) + (sds((2 * T, W), BF),) * 3,
        (out0, back1, back2, back3, halves),
        spaces=[VM] * 4 + [ANY],
    )
    f = [send_plane(parts[r - 1], -r, 0) for r in (1, 2, 3)]
    return call(
        last_kernel,
        "last",
        (sds((W, W), F32), sds((T, W), F32), sds((T, W), F32)),
        (u, part0, *f),
    )


def solution(mesh):
    fine = Mesh(mesh.devices.reshape(4, 4, 2, 4, 2), ("zl", "y", "core", "x", "zh"))
    qs, ks = ("x", "zh", "zl", "y", "core"), ("zl", "y", "core", "x", "zh")
    return jax.shard_map(
        local,
        mesh=fine,
        in_specs=(P(qs, None), P(ks, None), P(ks, None), P(qs, None), P(qs, None), P(qs)),
        out_specs=(P(qs, None), P(ks, None), P(ks, None)),
        check_vma=False,
    )
```

```python
import math

import jax
import jax.numpy as jnp
from jax import lax
from jax.experimental import pallas as pl
from jax.experimental.pallas import tpu as pltpu
from jax.sharding import Mesh, PartitionSpec as P

W = 128
JOIN_COST = 30_000_000_000
T = 240
QP = 2 * W + 16
BF, F32 = jnp.bfloat16, jnp.float32
FACTOR = 1.0 / math.sqrt(W)
LOG2E = math.log2(math.e)
NT = (((1,), (1,)), ((), ()))
NN = (((1,), (0,)), ((), ()))
TN = (((0,), (0,)), ((), ()))
VM = pl.BlockSpec(memory_space=pltpu.VMEM)
ANY = pl.BlockSpec(memory_space=pl.ANY)


def dot(a, b, dims):
    return lax.dot_general(a, b, dims, preferred_element_type=F32)


def call(kernel, name, outs, args, flops=0, aliases=None, spaces=None, scratch=(), vmem=40):
    nbytes = sum(math.prod(a.shape) * a.dtype.itemsize for a in list(outs) + list(args))
    return pl.pallas_call(
        kernel,
        name=name,
        out_shape=outs,
        in_specs=spaces or [VM] * len(args),
        out_specs=tuple([VM] * len(outs)),
        input_output_aliases=aliases or {},
        scratch_shapes=list(scratch),
        compiler_params=pltpu.CompilerParams(vmem_limit_bytes=vmem * 2**20),
        cost_estimate=pl.CostEstimate(flops=flops, bytes_accessed=nbytes, transcendentals=0),
    )(*args)


def sds(shape, dtype):
    return jax.ShapeDtypeStruct(shape, dtype)


def pack_kernel(q, g, o, lse, k, v, qp, kv, qbuf, gbuf, obuf, lbuf, sems):
    moves = (
        (g, gbuf),
        (o, obuf),
        (lse, lbuf),
        (q, qbuf),
        (k, kv.at[pl.ds(0, T), :]),
        (v, kv.at[pl.ds(T, T), :]),
    )
    copies = [pltpu.make_async_copy(src, dst, sems.at[n]) for n, (src, dst) in enumerate(moves)]
    for copy in copies:
        copy.start()
    for copy in copies[:3]:
        copy.wait()
    prod = gbuf[...].astype(F32) * obuf[...].astype(F32)
    delta = jnp.sum(prod.T, axis=0, keepdims=True)
    rows = []
    for x in (lbuf[...] * LOG2E, delta):
        for _ in range(3):
            part = x.astype(BF).astype(F32)
            rows.append(part)
            x = x - part
    rows.append(jnp.zeros((10, W), F32))
    stat = jnp.concatenate(rows, axis=0).astype(BF)
    for copy in copies[3:]:
        copy.wait()
    for z in range(8):
        qp[z, 0:W, :] = qbuf[...]
        qp[z, W : 2 * W, :] = gbuf[...]
        qp[z, 2 * W :, :] = stat


def join_kernel(k0, k1, k2, k3, out):
    for n, k in enumerate((k0, k1, k2, k3)):
        out[n] = k[...]


def after_kernel(x, after1, after2, out):
    out[...] = x[...]


def tiles_kernel(nq, jobs, touched, given, refs):
    qrefs, refs = refs[:nq], refs[nq:]
    kvs, refs = refs[: len(jobs)], refs[len(jobs) :]
    accs = dict(zip(given, refs))
    parts = list(refs[len(given) :])
    refs = refs[len(refs) - len(jobs) - len(touched) :]
    outs, sums = refs[: len(jobs)], dict(zip(touched, refs[len(jobs) :]))
    for kv, out, (sets, has_part) in zip(kvs, outs, jobs):
        part = parts.pop(0) if has_part else None
        ks = jnp.concatenate([kv[i, 0:T, :] for i in range(4)], axis=0)
        vs = jnp.concatenate([kv[i, T:, :] for i in range(4)], axis=0)
        gk = gv = None
        for r, at in [(r, at) for r in sets for at in (0, 4)]:
            mem = range(at, at + 4)
            q = jnp.concatenate([qrefs[r][i, 0:W, :] for i in mem], axis=0)
            g = jnp.concatenate([qrefs[r][i, W : 2 * W, :] for i in mem], axis=0)
            stat = jnp.concatenate([qrefs[r][i, 2 * W :, :].astype(F32) for i in mem], axis=1)
            l2 = stat[0:1] + stat[1:2] + stat[2:3]
            delta = stat[3:4] + stat[4:5] + stat[5:6]
            p = jnp.exp2(dot(ks, q, NT) * (FACTOR * LOG2E) - l2)
            ds = (p * (dot(vs, g, NT) - delta)).astype(BF)
            dv = dot(p.astype(BF), g, NN)
            dk = dot(ds, q, NN)
            gv = dv if gv is None else gv + dv
            gk = dk if gk is None else gk + dk
            u = dot(ks, ds, TN)
            for n, i in enumerate(mem):
                block = u[:, n * W : (n + 1) * W]
                sums[r][i] = accs[r][i] + block if r in accs else block
        for r in sets:
            accs[r] = sums[r]
        for i in range(4):
            rows = slice(i * T, (i + 1) * T)
            for col, total in ((slice(0, T), gk), (slice(T, 2 * T), gv)):
                block = total[rows]
                if has_part:
                    block = part[i, col, :] + block
                out[i, col, :] = block.astype(out.dtype)


def tiles(name, queries, jobs, acc, after=()):
    touched = sorted({r for _, sets, _, _ in jobs for r in sets})
    given = [r for r in touched if r in acc]
    outs = tuple(sds((4, 2 * T, W), dtype) for _, _, dtype, _ in jobs)
    outs += (sds((8, W, W), F32),) * len(touched)
    args = tuple(queries) + tuple(job[0] for job in jobs)
    aliases = {len(args) + n: len(jobs) + touched.index(r) for n, r in enumerate(given)}
    args += tuple(acc[r] for r in given)
    for n, job in enumerate(jobs):
        if job[3] is not None:
            if job[2] == F32:
                aliases[len(args)] = n
            args += (job[3],)
    spaces = [VM] * len(args) + [ANY] * len(after)
    args += tuple(after)
    static = [(sets, part is not None) for _, sets, _, part in jobs]

    def kernel(*refs):
        ins = refs[: len(args) - len(after)]
        tiles_kernel(len(queries), static, touched, given, ins + refs[len(args) :])

    flops = sum(10 * 960 * 1024 * len(sets) * W for sets, _ in static)
    out = call(kernel, name, outs, args, flops, aliases, spaces)
    return out[: len(jobs)], {**acc, **dict(zip(touched, out[len(jobs) :]))}


def merge_kernel(own, b1, b2, b3, after, *outs):
    for r in range(4):
        total = own[r]
        for other in (b1, b2, b3):
            total = total + other[r].astype(F32)
        outs[r][...] = total.astype(outs[r].dtype)


def halves_kernel(mine, got, out):
    out[...] = (mine[...] + got[...]).astype(BF)


def last_kernel(u, own, f1, f2, f3, gq, gk, gv):
    total = u[0].astype(F32)
    for z in range(1, 8):
        total = total + u[z].astype(F32)
    gq[...] = total.T * FACTOR
    total = own[...] + f1[...].astype(F32) + f2[...].astype(F32) + f3[...].astype(F32)
    gk[...] = total[0:T] * FACTOR
    gv[...] = total[T:]


SWAP = [(0, 1), (1, 0)]


def swap_cores(x):
    return lax.ppermute(x, "core", SWAP)


def exchange_z(x):
    return lax.all_to_all(x, ("zl", "zh"), 0, 0, tiled=True)


def send_plane(x, s, core_on_x):
    pairs = []
    for y in range(4):
        for c in range(2):
            for i in range(4):
                to_y, to_x = (y, (i + s) % 4) if c == core_on_x else ((y + s) % 4, i)
                pairs.append(((y * 2 + c) * 4 + i, (to_y * 2 + c) * 4 + to_x))
    return lax.ppermute(x, ("y", "core", "x"), pairs)


def local(queries, keys, values, outputs, out_grad, lse):
    qp, kv = call(
        pack_kernel,
        "pack",
        (sds((8, QP, W), BF), sds((2 * T, W), BF)),
        (queries, out_grad, outputs, lse.reshape(1, W), keys, values),
        spaces=[ANY] * 6,
        scratch=(
            pltpu.VMEM((W, W), BF),
            pltpu.VMEM((W, W), BF),
            pltpu.VMEM((W, W), BF),
            pltpu.VMEM((1, W), F32),
            pltpu.SemaphoreType.DMA((6,)),
        ),
        vmem=60,
    )
    same = exchange_z(qp)
    (kv0,) = call(
        join_kernel,
        "join",
        (sds((4, 2 * T, W), BF),),
        (kv, *(send_plane(kv, r, 0) for r in (1, 2, 3))),
        flops=JOIN_COST,
    )
    kv1, kv3, kv2 = (send_plane(kv0, s, 1) for s in (1, 3, 2))
    (same,) = call(after_kernel, "same", (sds((8, QP, W), BF),), (same, kv1, kv3), spaces=[VM, ANY, ANY])

    qs = (same, swap_cores(same))
    (part1, part3), acc = tiles(
        "tiles13a", qs[:1], ((kv1, (0,), F32, None), (kv3, (0,), F32, None)), {}
    )
    (out1, out3, part0), acc = tiles(
        "tiles130",
        qs,
        ((kv1, (1,), BF, part1), (kv3, (1,), BF, part3), (kv0, (1,), F32, None)),
        acc,
    )
    back1, back3 = send_plane(out1, -1, 1), send_plane(out3, -3, 1)
    (out2,), acc = tiles("tiles2", qs, ((kv2, (0, 1), BF, None),), acc)
    rs, back2 = swap_cores(acc[1]), send_plane(out2, -2, 1)
    (out0,), acc = tiles("tiles0", qs, ((kv0, (0,), F32, part0),), acc, (back1, back3))

    (halves,) = call(halves_kernel, "halves", (sds((8, W, W), BF),), (acc[0], rs))
    u = exchange_z(halves)
    part0, *parts = call(
        merge_kernel,
        "merge",
        (sds((2 * T, W), F32),) + (sds((2 * T, W), BF),) * 3,
        (out0, back1, back2, back3, halves),
        spaces=[VM] * 4 + [ANY],
    )
    f = [send_plane(parts[r - 1], -r, 0) for r in (1, 2, 3)]
    return call(
        last_kernel,
        "last",
        (sds((W, W), F32), sds((T, W), F32), sds((T, W), F32)),
        (u, part0, *f),
    )


def solution(mesh):
    fine = Mesh(mesh.devices.reshape(4, 4, 2, 4, 2), ("zl", "y", "core", "x", "zh"))
    qs, ks = ("x", "zh", "zl", "y", "core"), ("zl", "y", "core", "x", "zh")
    return jax.shard_map(
        local,
        mesh=fine,
        in_specs=(P(qs, None), P(ks, None), P(ks, None), P(qs, None), P(qs, None), P(qs)),
        out_specs=(P(qs, None), P(ks, None), P(ks, None)),
        check_vma=False,
    )
```

```python
import math

import jax
import jax.numpy as jnp
from jax import lax
from jax.experimental import pallas as pl
from jax.experimental.pallas import tpu as pltpu
from jax.sharding import Mesh, PartitionSpec as P

W = 128
JOIN_COST = 20_000_000_000
FIRST_COST = 20_000_000_000
CHIP_COST = 20_000_000_000
T = 240
QP = 2 * W + 16
BF, F32 = jnp.bfloat16, jnp.float32
FACTOR = 1.0 / math.sqrt(W)
LOG2E = math.log2(math.e)
NT = (((1,), (1,)), ((), ()))
NN = (((1,), (0,)), ((), ()))
TN = (((0,), (0,)), ((), ()))
VM = pl.BlockSpec(memory_space=pltpu.VMEM)
ANY = pl.BlockSpec(memory_space=pl.ANY)


def dot(a, b, dims):
    return lax.dot_general(a, b, dims, preferred_element_type=F32)


def call(kernel, name, outs, args, flops=0, aliases=None, spaces=None, scratch=(), vmem=40):
    nbytes = sum(math.prod(a.shape) * a.dtype.itemsize for a in list(outs) + list(args))
    return pl.pallas_call(
        kernel,
        name=name,
        out_shape=outs,
        in_specs=spaces or [VM] * len(args),
        out_specs=tuple([VM] * len(outs)),
        input_output_aliases=aliases or {},
        scratch_shapes=list(scratch),
        compiler_params=pltpu.CompilerParams(vmem_limit_bytes=vmem * 2**20),
        cost_estimate=pl.CostEstimate(flops=flops, bytes_accessed=nbytes, transcendentals=0),
    )(*args)


def sds(shape, dtype):
    return jax.ShapeDtypeStruct(shape, dtype)


def pack_kernel(q, g, o, lse, k, v, qp, kv, qbuf, gbuf, obuf, lbuf, sems):
    moves = (
        (g, gbuf),
        (o, obuf),
        (lse, lbuf),
        (q, qbuf),
        (k, kv.at[pl.ds(0, T), :]),
        (v, kv.at[pl.ds(T, T), :]),
    )
    copies = [pltpu.make_async_copy(src, dst, sems.at[n]) for n, (src, dst) in enumerate(moves)]
    for copy in copies:
        copy.start()
    for copy in copies[:3]:
        copy.wait()
    prod = gbuf[...].astype(F32) * obuf[...].astype(F32)
    delta = jnp.sum(prod.T, axis=0, keepdims=True)
    rows = []
    for x in (lbuf[...] * LOG2E, delta):
        for _ in range(3):
            part = x.astype(BF).astype(F32)
            rows.append(part)
            x = x - part
    rows.append(jnp.zeros((10, W), F32))
    stat = jnp.concatenate(rows, axis=0).astype(BF)
    for copy in copies[3:]:
        copy.wait()
    qp[0:W, :] = qbuf[...]
    qp[W : 2 * W, :] = gbuf[...]
    qp[2 * W :, :] = stat


def pair_kernel(q0, q1, out):
    out[0] = q0[...]
    out[1] = q1[...]


def join_kernel(k0, k1, k2, k3, out):
    for n, k in enumerate((k0, k1, k2, k3)):
        out[n] = k[...]


def after_kernel(x, after, out):
    out[...] = x[...]


def first_kernel(q, out):
    out[...] = q[0:1]


def gather_kernel(q1, q2, q3, q4, kv1, kv3, out):
    for n, q in enumerate((q1, q2, q3)):
        out[2 * n : 2 * n + 2] = q[...]
    out[6:7] = q4[...]


GROUPS = (
    ((0, 0), (1, 0), (1, 2), (1, 4)),
    ((1, 6), (2, 1), (2, 3), (2, 5)),
    ((0, 1), (1, 1), (1, 3), (1, 5)),
    ((2, 0), (2, 2), (2, 4), (2, 6)),
)
UP = (0, -1, -2, -3, -4, 1, 2, 3)
TWIN = (0, 4, 5, 6, 7, 1, 2, 3)


def tiles_kernel(nq, jobs, touched, given, refs):
    qrefs, refs = refs[:nq], refs[nq:]
    kvs, refs = refs[: len(jobs)], refs[len(jobs) :]
    accs = dict(zip(given, refs))
    parts = list(refs[len(given) :])
    refs = refs[len(refs) - len(jobs) - len(touched) :]
    outs, sums = refs[: len(jobs)], dict(zip(touched, refs[len(jobs) :]))
    for kv, out, (sets, has_part) in zip(kvs, outs, jobs):
        part = parts.pop(0) if has_part else None
        ks = jnp.concatenate([kv[i, 0:T, :] for i in range(4)], axis=0)
        vs = jnp.concatenate([kv[i, T:, :] for i in range(4)], axis=0)
        gk = gv = None
        for c in sets:
            mem = GROUPS[c]
            q = jnp.concatenate([qrefs[r][i, 0:W, :] for r, i in mem], axis=0)
            g = jnp.concatenate([qrefs[r][i, W : 2 * W, :] for r, i in mem], axis=0)
            stat = jnp.concatenate([qrefs[r][i, 2 * W :, :].astype(F32) for r, i in mem], axis=1)
            l2 = stat[0:1] + stat[1:2] + stat[2:3]
            delta = stat[3:4] + stat[4:5] + stat[5:6]
            p = jnp.exp2(dot(ks, q, NT) * (FACTOR * LOG2E) - l2)
            ds = (p * (dot(vs, g, NT) - delta)).astype(BF)
            dv = dot(p.astype(BF), g, NN)
            dk = dot(ds, q, NN)
            gv = dv if gv is None else gv + dv
            gk = dk if gk is None else gk + dk
            u = dot(ks, ds, TN)
            for n in range(4):
                block = u[:, n * W : (n + 1) * W]
                sums[c][n] = accs[c][n] + block if c in accs else block
            accs[c] = sums[c]
        for i in range(4):
            rows = slice(i * T, (i + 1) * T)
            for col, total in ((slice(0, T), gk), (slice(T, 2 * T), gv)):
                block = total[rows]
                if has_part:
                    block = part[i, col, :] + block
                out[i, col, :] = block.astype(out.dtype)


def tiles(name, queries, jobs, acc, after=()):
    touched = sorted({c for _, sets, _, _ in jobs for c in sets})
    given = [r for r in touched if r in acc]
    outs = tuple(sds((4, 2 * T, W), dtype) for _, _, dtype, _ in jobs)
    outs += (sds((4, W, W), F32),) * len(touched)
    args = tuple(queries) + tuple(job[0] for job in jobs)
    aliases = {len(args) + n: len(jobs) + touched.index(r) for n, r in enumerate(given)}
    args += tuple(acc[r] for r in given)
    for n, job in enumerate(jobs):
        if job[3] is not None:
            if job[2] == F32:
                aliases[len(args)] = n
            args += (job[3],)
    spaces = [VM] * len(args) + [ANY] * len(after)
    args += tuple(after)
    static = [(sets, part is not None) for _, sets, _, part in jobs]

    def kernel(*refs):
        ins = refs[: len(args) - len(after)]
        tiles_kernel(len(queries), static, touched, given, ins + refs[len(args) :])

    flops = sum(10 * 960 * 512 * len(sets) * W for sets, _ in static)
    out = call(kernel, name, outs, args, flops, aliases, spaces)
    return out[: len(jobs)], {**acc, **dict(zip(touched, out[len(jobs) :]))}


def stack_kernel(a, b, out):
    out[0:4] = a[...]
    out[4:8] = b[...]


def merge_kernel(own, b1, b2, b3, after, *outs):
    for r in range(4):
        total = own[r]
        for other in (b1, b2, b3):
            total = total + other[r].astype(F32)
        outs[r][...] = total.astype(outs[r].dtype)


def halves_kernel(near, far, got, out):
    up = 1 - 2 * lax.axis_index("core")
    here = 4 * lax.axis_index("zh") + lax.axis_index("zl") + 8
    for n in range(8):
        z = lax.rem(here + up * UP[n], 8)
        mine = near[n] if n < 4 else far[n - 4]
        out[2 * lax.rem(z, 4) + z // 4] = (mine + got[TWIN[n]]).astype(BF)


def last_kernel(u, own, f1, f2, f3, gq, gk, gv):
    total = u[0].astype(F32)
    for z in range(1, 8):
        total = total + u[z].astype(F32)
    gq[...] = total.T * FACTOR
    total = own[...] + f1[...].astype(F32) + f2[...].astype(F32) + f3[...].astype(F32)
    gk[...] = total[0:T] * FACTOR
    gv[...] = total[T:]


SWAP = [(0, 1), (1, 0)]


def swap_cores(x):
    return lax.ppermute(x, "core", SWAP)


def send_z(x, s):
    index = lambda z, c: (z % 4) * 4 + c * 2 + z // 4
    pairs = [
        (index(z, c), index((z + (s if c == 0 else -s)) % 8, c)) for z in range(8) for c in range(2)
    ]
    return lax.ppermute(x, ("zl", "core", "zh"), pairs)


def exchange_z(x):
    return lax.all_to_all(x, ("zl", "zh"), 0, 0, tiled=True)


def send_plane(x, s, core_on_x):
    pairs = []
    for y in range(4):
        for c in range(2):
            for i in range(4):
                to_y, to_x = (y, (i + s) % 4) if c == core_on_x else ((y + s) % 4, i)
                pairs.append(((y * 2 + c) * 4 + i, (to_y * 2 + c) * 4 + to_x))
    return lax.ppermute(x, ("y", "core", "x"), pairs)


def local(queries, keys, values, outputs, out_grad, lse):
    qp, kv = call(
        pack_kernel,
        "pack",
        (sds((QP, W), BF), sds((2 * T, W), BF)),
        (queries, out_grad, outputs, lse.reshape(1, W), keys, values),
        spaces=[ANY] * 6,
        scratch=(
            pltpu.VMEM((W, W), BF),
            pltpu.VMEM((W, W), BF),
            pltpu.VMEM((W, W), BF),
            pltpu.VMEM((1, W), F32),
            pltpu.SemaphoreType.DMA((6,)),
        ),
        vmem=60,
    )
    ks = [send_plane(kv, r, 0) for r in (1, 2, 3)]
    (chip,) = call(pair_kernel, "chip", (sds((2, QP, W), BF),), (qp, swap_cores(qp)), CHIP_COST)
    (kv0,) = call(join_kernel, "join", (sds((4, 2 * T, W), BF),), (kv, *ks), JOIN_COST)
    kv1, kv3 = (send_plane(kv0, s, 1) for s in (1, 3))
    q1, q2 = send_z(chip, 1), send_z(chip, 2)
    (q2_own,) = call(first_kernel, "first", (sds((1, QP, W), BF),), (q2,), FIRST_COST)
    q3, q4 = send_z(q2, 1), send_z(q2_own, 2)
    (mine,) = call(
        gather_kernel,
        "gather",
        (sds((7, QP, W), BF),),
        (q1, q2, q3, q4, kv1, kv3),
        spaces=[VM] * 4 + [ANY] * 2,
    )
    (kv0_late,) = call(
        after_kernel, "late", (sds((4, 2 * T, W), BF),), (kv0, mine), spaces=[VM, ANY]
    )
    kv2 = send_plane(kv0_late, 2, 1)

    qs = (chip, mine, swap_cores(mine))
    (part1, part3), acc = tiles(
        "tiles13a", qs[:2], ((kv1, (0, 2), F32, None), (kv3, (0, 2), F32, None)), {}
    )
    (out1, out3, part0), acc = tiles(
        "tiles130",
        qs,
        ((kv1, (1, 3), BF, part1), (kv3, (1, 3), BF, part3), (kv0, (2, 3), F32, None)),
        acc,
    )
    back1, back3 = send_plane(out1, -1, 1), send_plane(out3, -3, 1)
    (out2,), acc = tiles("tiles2", qs, ((kv2, (0, 1, 2, 3), BF, None),), acc)
    (others,) = call(stack_kernel, "others", (sds((8, W, W), F32),), (acc[2], acc[3]))
    rs, back2 = swap_cores(others), send_plane(out2, -2, 1)
    (out0,), acc = tiles("tiles0", qs, ((kv0, (0, 1), F32, part0),), acc, (back1, back3))

    (halves,) = call(halves_kernel, "halves", (sds((8, W, W), BF),), (acc[0], acc[1], rs))
    u = exchange_z(halves)
    part0, *parts = call(
        merge_kernel,
        "merge",
        (sds((2 * T, W), F32),) + (sds((2 * T, W), BF),) * 3,
        (out0, back1, back2, back3, halves),
        spaces=[VM] * 4 + [ANY],
    )
    f = [send_plane(parts[r - 1], -r, 0) for r in (1, 2, 3)]
    return call(
        last_kernel,
        "last",
        (sds((W, W), F32), sds((T, W), F32), sds((T, W), F32)),
        (u, part0, *f),
    )


def solution(mesh):
    fine = Mesh(mesh.devices.reshape(4, 4, 2, 4, 2), ("zl", "y", "core", "x", "zh"))
    qs, ks = ("x", "zh", "zl", "y", "core"), ("zl", "y", "core", "x", "zh")
    return jax.shard_map(
        local,
        mesh=fine,
        in_specs=(P(qs, None), P(ks, None), P(ks, None), P(qs, None), P(qs, None), P(qs)),
        out_specs=(P(qs, None), P(ks, None), P(ks, None)),
        check_vma=False,
    )
```

```python
import math

import jax
import jax.numpy as jnp
from jax import lax
from jax.experimental import pallas as pl
from jax.experimental.pallas import tpu as pltpu
from jax.sharding import Mesh, PartitionSpec as P

W = 128
JOIN_COST = 20_000_000_000
FIRST_COST = 20_000_000_000
CHIP_COST = 20_000_000_000
T = 240
QP = 2 * W + 16
BF, F32 = jnp.bfloat16, jnp.float32
FACTOR = 1.0 / math.sqrt(W)
LOG2E = math.log2(math.e)
NT = (((1,), (1,)), ((), ()))
NN = (((1,), (0,)), ((), ()))
TN = (((0,), (0,)), ((), ()))
VM = pl.BlockSpec(memory_space=pltpu.VMEM)
ANY = pl.BlockSpec(memory_space=pl.ANY)


def dot(a, b, dims):
    return lax.dot_general(a, b, dims, preferred_element_type=F32)


def call(kernel, name, outs, args, flops=0, aliases=None, spaces=None, scratch=(), vmem=40):
    nbytes = sum(math.prod(a.shape) * a.dtype.itemsize for a in list(outs) + list(args))
    return pl.pallas_call(
        kernel,
        name=name,
        out_shape=outs,
        in_specs=spaces or [VM] * len(args),
        out_specs=tuple([VM] * len(outs)),
        input_output_aliases=aliases or {},
        scratch_shapes=list(scratch),
        compiler_params=pltpu.CompilerParams(vmem_limit_bytes=vmem * 2**20),
        cost_estimate=pl.CostEstimate(flops=flops, bytes_accessed=nbytes, transcendentals=0),
    )(*args)


def sds(shape, dtype):
    return jax.ShapeDtypeStruct(shape, dtype)


def pack_kernel(q, g, o, lse, k, v, qp, kv, qbuf, gbuf, obuf, lbuf, sems):
    moves = (
        (g, gbuf),
        (o, obuf),
        (lse, lbuf),
        (q, qbuf),
        (k, kv.at[pl.ds(0, T), :]),
        (v, kv.at[pl.ds(T, T), :]),
    )
    copies = [pltpu.make_async_copy(src, dst, sems.at[n]) for n, (src, dst) in enumerate(moves)]
    for copy in copies:
        copy.start()
    for copy in copies[:3]:
        copy.wait()
    prod = gbuf[...].astype(F32) * obuf[...].astype(F32)
    delta = jnp.sum(prod.T, axis=0, keepdims=True)
    rows = []
    for x in (lbuf[...] * LOG2E, delta):
        for _ in range(3):
            part = x.astype(BF).astype(F32)
            rows.append(part)
            x = x - part
    rows.append(jnp.zeros((10, W), F32))
    stat = jnp.concatenate(rows, axis=0).astype(BF)
    for copy in copies[3:]:
        copy.wait()
    qp[0:W, :] = qbuf[...]
    qp[W : 2 * W, :] = gbuf[...]
    qp[2 * W :, :] = stat


def pair_kernel(q0, q1, out):
    out[0] = q0[...]
    out[1] = q1[...]


def join_kernel(k0, k1, k2, k3, out):
    for n, k in enumerate((k0, k1, k2, k3)):
        out[n] = k[...]


def after_kernel(x, after, out):
    out[...] = x[...]


def first_kernel(q, out):
    out[...] = q[0:1]


def gather_kernel(q1, q2, q3, q4, kv1, kv3, part, out):
    for n, q in enumerate((q1, q2, q3)):
        out[2 * n : 2 * n + 2] = q[...]
    out[6:7] = q4[...]


GROUPS = (
    ((0, 1), (1, 1), (1, 3), (0, 0)),
    ((1, 0), (1, 2), (1, 4), (1, 5)),
    ((1, 6), (2, 1), (2, 3), (2, 5)),
    ((2, 0), (2, 2), (2, 4), (2, 6)),
    ((0, 1), (3, 1), (4, 1), (0, 0)),
)
SAME = ((0, 3), (1, 0), (1, 1), (1, 2), (2, 0), (2, 1), (2, 2), (2, 3))
UP = (0, -1, -2, -3, -4, 1, 2, 3)
TWIN = (0, 4, 5, 6, 7, 1, 2, 3)


def tiles_kernel(ops, jobs, touched, given, refs):
    qrefs, refs = dict(zip(ops, refs)), refs[len(ops) :]
    kvs, refs = refs[: len(jobs)], refs[len(jobs) :]
    accs = dict(zip(given, refs))
    parts = list(refs[len(given) :])
    refs = refs[len(refs) - len(jobs) - len(touched) :]
    outs, sums = refs[: len(jobs)], dict(zip(touched, refs[len(jobs) :]))
    for kv, out, (sets, has_part) in zip(kvs, outs, jobs):
        part = parts.pop(0) if has_part else None
        ks = jnp.concatenate([kv[i, 0:T, :] for i in range(4)], axis=0)
        vs = jnp.concatenate([kv[i, T:, :] for i in range(4)], axis=0)
        gk = gv = None
        for c in sets:
            mem = GROUPS[c]
            q = jnp.concatenate([qrefs[r][i, 0:W, :] for r, i in mem], axis=0)
            g = jnp.concatenate([qrefs[r][i, W : 2 * W, :] for r, i in mem], axis=0)
            stat = jnp.concatenate([qrefs[r][i, 2 * W :, :].astype(F32) for r, i in mem], axis=1)
            l2 = stat[0:1] + stat[1:2] + stat[2:3]
            delta = stat[3:4] + stat[4:5] + stat[5:6]
            p = jnp.exp2(dot(ks, q, NT) * (FACTOR * LOG2E) - l2)
            ds = (p * (dot(vs, g, NT) - delta)).astype(BF)
            dv = dot(p.astype(BF), g, NN)
            dk = dot(ds, q, NN)
            gv = dv if gv is None else gv + dv
            gk = dk if gk is None else gk + dk
            u = dot(ks, ds, TN)
            c = c % 4
            for n in range(4):
                block = u[:, n * W : (n + 1) * W]
                sums[c][n] = accs[c][n] + block if c in accs else block
            accs[c] = sums[c]
        for i in range(4):
            rows = slice(i * T, (i + 1) * T)
            for col, total in ((slice(0, T), gk), (slice(T, 2 * T), gv)):
                block = total[rows]
                if has_part:
                    block = part[i, col, :] + block
                out[i, col, :] = block.astype(out.dtype)


def tiles(name, queries, jobs, acc, after=()):
    touched = sorted({c % 4 for _, sets, _, _ in jobs for c in sets})
    given = [r for r in touched if r in acc]
    outs = tuple(sds((4, 2 * T, W), dtype) for _, _, dtype, _ in jobs)
    outs += (sds((4, W, W), F32),) * len(touched)
    args = tuple(queries.values()) + tuple(job[0] for job in jobs)
    aliases = {len(args) + n: len(jobs) + touched.index(r) for n, r in enumerate(given)}
    args += tuple(acc[r] for r in given)
    for n, job in enumerate(jobs):
        if job[3] is not None:
            if job[2] == F32:
                aliases[len(args)] = n
            args += (job[3],)
    spaces = [VM] * len(args) + [ANY] * len(after)
    args += tuple(after)
    static = [(sets, part is not None) for _, sets, _, part in jobs]

    def kernel(*refs):
        ins = refs[: len(args) - len(after)]
        tiles_kernel(tuple(queries), static, touched, given, ins + refs[len(args) :])

    flops = sum(10 * 960 * 512 * len(sets) * W for sets, _ in static)
    out = call(kernel, name, outs, args, flops, aliases, spaces)
    return out[: len(jobs)], {**acc, **dict(zip(touched, out[len(jobs) :]))}


def stack_kernel(g0, g1, g3, out):
    out[0:3] = g0[0:3]
    out[3] = g1[3]
    out[4:8] = g3[...]


def merge_kernel(own, b1, b2, b3, after, *outs):
    for r in range(4):
        total = own[r]
        for other in (b1, b2, b3):
            total = total + other[r].astype(F32)
        outs[r][...] = total.astype(outs[r].dtype)


def halves_kernel(g0, g1, g2, got, out):
    groups = (g0, g1, g2)
    up = 1 - 2 * lax.axis_index("core")
    here = 4 * lax.axis_index("zh") + lax.axis_index("zl") + 8
    for n, (group, place) in enumerate(SAME):
        z = lax.rem(here + up * UP[n], 8)
        out[2 * lax.rem(z, 4) + z // 4] = (groups[group][place] + got[TWIN[n]]).astype(BF)


def last_kernel(u, own, f1, f2, f3, gq, gk, gv):
    total = u[0].astype(F32)
    for z in range(1, 8):
        total = total + u[z].astype(F32)
    gq[...] = total.T * FACTOR
    total = own[...] + f1[...].astype(F32) + f2[...].astype(F32) + f3[...].astype(F32)
    gk[...] = total[0:T] * FACTOR
    gv[...] = total[T:]


SWAP = [(0, 1), (1, 0)]


def swap_cores(x):
    return lax.ppermute(x, "core", SWAP)


def send_z(x, s):
    index = lambda z, c: (z % 4) * 4 + c * 2 + z // 4
    pairs = [
        (index(z, c), index((z + (s if c == 0 else -s)) % 8, c)) for z in range(8) for c in range(2)
    ]
    return lax.ppermute(x, ("zl", "core", "zh"), pairs)


def exchange_z(x):
    return lax.all_to_all(x, ("zl", "zh"), 0, 0, tiled=True)


def send_plane(x, s, core_on_x):
    pairs = []
    for y in range(4):
        for c in range(2):
            for i in range(4):
                to_y, to_x = (y, (i + s) % 4) if c == core_on_x else ((y + s) % 4, i)
                pairs.append(((y * 2 + c) * 4 + i, (to_y * 2 + c) * 4 + to_x))
    return lax.ppermute(x, ("y", "core", "x"), pairs)


def local(queries, keys, values, outputs, out_grad, lse):
    qp, kv = call(
        pack_kernel,
        "pack",
        (sds((QP, W), BF), sds((2 * T, W), BF)),
        (queries, out_grad, outputs, lse.reshape(1, W), keys, values),
        spaces=[ANY] * 6,
        scratch=(
            pltpu.VMEM((W, W), BF),
            pltpu.VMEM((W, W), BF),
            pltpu.VMEM((W, W), BF),
            pltpu.VMEM((1, W), F32),
            pltpu.SemaphoreType.DMA((6,)),
        ),
        vmem=60,
    )
    ks = [send_plane(kv, r, 0) for r in (1, 2, 3)]
    (chip,) = call(pair_kernel, "chip", (sds((2, QP, W), BF),), (qp, swap_cores(qp)), CHIP_COST)
    (kv0,) = call(join_kernel, "join", (sds((4, 2 * T, W), BF),), (kv, *ks), JOIN_COST)
    kv1, kv3 = (send_plane(kv0, s, 1) for s in (1, 3))
    q1, q2 = send_z(chip, 1), send_z(chip, 2)
    (q2_own,) = call(first_kernel, "first", (sds((1, QP, W), BF),), (q2,), FIRST_COST)
    q3, q4 = send_z(q2, 1), send_z(q2_own, 2)
    (part0,), acc = tiles("tiles0e", {0: chip, 3: q1, 4: q2}, ((kv0, (4,), F32, None),), {})
    (mine,) = call(
        gather_kernel,
        "gather",
        (sds((7, QP, W), BF),),
        (q1, q2, q3, q4, kv1, kv3, part0),
        spaces=[VM] * 4 + [ANY] * 3,
    )
    (kv0_late,) = call(
        after_kernel, "late", (sds((4, 2 * T, W), BF),), (kv0, mine), spaces=[VM, ANY]
    )
    kv2 = send_plane(kv0_late, 2, 1)

    sib = swap_cores(mine)
    (part1, part3), acc = tiles(
        "tiles13a",
        {0: chip, 1: mine},
        ((kv1, (0, 1), F32, None), (kv3, (0, 1), F32, None)),
        acc,
    )
    qs = {0: chip, 1: mine, 2: sib}
    (out1, out3, part0), acc = tiles(
        "tiles130",
        qs,
        ((kv1, (2, 3), BF, part1), (kv3, (2, 3), BF, part3), (kv0, (1, 3), F32, part0)),
        acc,
    )
    back1, back3 = send_plane(out1, -1, 1), send_plane(out3, -3, 1)
    (out2,), acc = tiles("tiles2", qs, ((kv2, (0, 1, 2, 3), BF, None),), acc)
    (others,) = call(stack_kernel, "others", (sds((8, W, W), F32),), (acc[0], acc[1], acc[3]))
    rs, back2 = swap_cores(others), send_plane(out2, -2, 1)
    (out0,), acc = tiles("tiles0", qs, ((kv0, (2,), F32, part0),), acc, (back1, back3))

    (halves,) = call(halves_kernel, "halves", (sds((8, W, W), BF),), (acc[0], acc[1], acc[2], rs))
    u = exchange_z(halves)
    part0, *parts = call(
        merge_kernel,
        "merge",
        (sds((2 * T, W), F32),) + (sds((2 * T, W), BF),) * 3,
        (out0, back1, back2, back3, halves),
        spaces=[VM] * 4 + [ANY],
    )
    f = [send_plane(parts[r - 1], -r, 0) for r in (1, 2, 3)]
    return call(
        last_kernel,
        "last",
        (sds((W, W), F32), sds((T, W), F32), sds((T, W), F32)),
        (u, part0, *f),
    )


def solution(mesh):
    fine = Mesh(mesh.devices.reshape(4, 4, 2, 4, 2), ("zl", "y", "core", "x", "zh"))
    qs, ks = ("x", "zh", "zl", "y", "core"), ("zl", "y", "core", "x", "zh")
    return jax.shard_map(
        local,
        mesh=fine,
        in_specs=(P(qs, None), P(ks, None), P(ks, None), P(qs, None), P(qs, None), P(qs)),
        out_specs=(P(qs, None), P(ks, None), P(ks, None)),
        check_vma=False,
    )
```

```python
import math

import jax
import jax.numpy as jnp
from jax import lax
from jax.experimental import pallas as pl
from jax.experimental.pallas import tpu as pltpu
from jax.sharding import Mesh, PartitionSpec as P

W = 128
JOIN_COST = 20_000_000_000
FIRST_COST = 20_000_000_000
CHIP_COST = 20_000_000_000
T = 240
QP = 2 * W + 16
BF, F32 = jnp.bfloat16, jnp.float32
FACTOR = 1.0 / math.sqrt(W)
LOG2E = math.log2(math.e)
NT = (((1,), (1,)), ((), ()))
NN = (((1,), (0,)), ((), ()))
TN = (((0,), (0,)), ((), ()))
VM = pl.BlockSpec(memory_space=pltpu.VMEM)
ANY = pl.BlockSpec(memory_space=pl.ANY)


def dot(a, b, dims):
    return lax.dot_general(a, b, dims, preferred_element_type=F32)


def call(kernel, name, outs, args, flops=0, aliases=None, spaces=None, scratch=(), vmem=40):
    nbytes = sum(math.prod(a.shape) * a.dtype.itemsize for a in list(outs) + list(args))
    return pl.pallas_call(
        kernel,
        name=name,
        out_shape=outs,
        in_specs=spaces or [VM] * len(args),
        out_specs=tuple([VM] * len(outs)),
        input_output_aliases=aliases or {},
        scratch_shapes=list(scratch),
        compiler_params=pltpu.CompilerParams(vmem_limit_bytes=vmem * 2**20),
        cost_estimate=pl.CostEstimate(flops=flops, bytes_accessed=nbytes, transcendentals=0),
    )(*args)


def sds(shape, dtype):
    return jax.ShapeDtypeStruct(shape, dtype)


def pack_kernel(q, g, o, lse, k, v, qp, kv, qbuf, gbuf, obuf, lbuf, sems):
    moves = (
        (g, gbuf),
        (o, obuf),
        (lse, lbuf),
        (q, qbuf),
        (k, kv.at[pl.ds(0, T), :]),
        (v, kv.at[pl.ds(T, T), :]),
    )
    copies = [pltpu.make_async_copy(src, dst, sems.at[n]) for n, (src, dst) in enumerate(moves)]
    for copy in copies:
        copy.start()
    for copy in copies[:3]:
        copy.wait()
    prod = gbuf[...].astype(F32) * obuf[...].astype(F32)
    delta = jnp.sum(prod.T, axis=0, keepdims=True)
    rows = []
    for x in (lbuf[...] * LOG2E, delta):
        for _ in range(3):
            part = x.astype(BF).astype(F32)
            rows.append(part)
            x = x - part
    rows.append(jnp.zeros((10, W), F32))
    stat = jnp.concatenate(rows, axis=0).astype(BF)
    for copy in copies[3:]:
        copy.wait()
    qp[0:W, :] = qbuf[...]
    qp[W : 2 * W, :] = gbuf[...]
    qp[2 * W :, :] = stat


def pair_kernel(q0, q1, out):
    out[0] = q0[...]
    out[1] = q1[...]


def join_kernel(k0, k1, k2, k3, out):
    for n, k in enumerate((k0, k1, k2, k3)):
        out[n] = k[...]


def after_kernel(x, after, out):
    out[...] = x[...]


def first_kernel(q, out):
    out[...] = q[0:1]


def gather_kernel(q1, q2, q3, q4, kv1, kv3, part, out):
    for n, q in enumerate((q1, q2, q3)):
        out[2 * n : 2 * n + 2] = q[...]
    out[6:7] = q4[...]


GROUPS = (
    ((0, 1), (1, 1), (1, 3), (0, 0)),
    ((1, 0), (1, 2), (1, 4), (1, 5)),
    ((1, 6), (2, 1), (2, 3), (2, 5)),
    ((2, 0), (2, 2), (2, 4), (2, 6)),
    ((0, 1), (3, 1), (4, 1), (0, 0)),
)
SAME = ((0, 3), (1, 0), (1, 1), (1, 2), (2, 0), (2, 1), (2, 2), (2, 3))
UP = (0, -1, -2, -3, -4, 1, 2, 3)
TWIN = (0, 4, 5, 6, 7, 1, 2, 3)


def tiles_kernel(ops, jobs, touched, given, refs):
    qrefs, refs = dict(zip(ops, refs)), refs[len(ops) :]
    kvs, refs = refs[: len(jobs)], refs[len(jobs) :]
    accs = dict(zip(given, refs))
    parts = list(refs[len(given) :])
    refs = refs[len(refs) - len(jobs) - len(touched) :]
    outs, sums = refs[: len(jobs)], dict(zip(touched, refs[len(jobs) :]))
    for kv, out, (sets, has_part) in zip(kvs, outs, jobs):
        part = parts.pop(0) if has_part else None
        ks = jnp.concatenate([kv[i, 0:T, :] for i in range(4)], axis=0)
        vs = jnp.concatenate([kv[i, T:, :] for i in range(4)], axis=0)
        gk = gv = None
        for c in sets:
            mem = GROUPS[c]
            q = jnp.concatenate([qrefs[r][i, 0:W, :] for r, i in mem], axis=0)
            g = jnp.concatenate([qrefs[r][i, W : 2 * W, :] for r, i in mem], axis=0)
            stat = jnp.concatenate([qrefs[r][i, 2 * W :, :].astype(F32) for r, i in mem], axis=1)
            l2 = stat[0:1] + stat[1:2] + stat[2:3]
            delta = stat[3:4] + stat[4:5] + stat[5:6]
            p = jnp.exp2(dot(ks, q, NT) * (FACTOR * LOG2E) - l2)
            ds = (p * (dot(vs, g, NT) - delta)).astype(BF)
            dv = dot(p.astype(BF), g, NN)
            dk = dot(ds, q, NN)
            gv = dv if gv is None else gv + dv
            gk = dk if gk is None else gk + dk
            u = dot(ks, ds, TN)
            c = c % 4
            for n in range(4):
                block = u[:, n * W : (n + 1) * W]
                sums[c][n] = accs[c][n] + block if c in accs else block
            accs[c] = sums[c]
        for i in range(4):
            rows = slice(i * T, (i + 1) * T)
            for col, total in ((slice(0, T), gk), (slice(T, 2 * T), gv)):
                block = total[rows]
                if has_part:
                    block = part[i, col, :] + block
                out[i, col, :] = block.astype(out.dtype)


def tiles(name, queries, jobs, acc, after=()):
    touched = sorted({c % 4 for _, sets, _, _ in jobs for c in sets})
    given = [r for r in touched if r in acc]
    outs = tuple(sds((4, 2 * T, W), dtype) for _, _, dtype, _ in jobs)
    outs += (sds((4, W, W), F32),) * len(touched)
    args = tuple(queries.values()) + tuple(job[0] for job in jobs)
    aliases = {len(args) + n: len(jobs) + touched.index(r) for n, r in enumerate(given)}
    args += tuple(acc[r] for r in given)
    for n, job in enumerate(jobs):
        if job[3] is not None:
            if job[2] == F32:
                aliases[len(args)] = n
            args += (job[3],)
    spaces = [VM] * len(args) + [ANY] * len(after)
    args += tuple(after)
    static = [(sets, part is not None) for _, sets, _, part in jobs]

    def kernel(*refs):
        ins = refs[: len(args) - len(after)]
        tiles_kernel(tuple(queries), static, touched, given, ins + refs[len(args) :])

    flops = sum(10 * 960 * 512 * len(sets) * W for sets, _ in static)
    out = call(kernel, name, outs, args, flops, aliases, spaces)
    return out[: len(jobs)], {**acc, **dict(zip(touched, out[len(jobs) :]))}


def stack_kernel(g0, g1, g3, out):
    out[0:3] = g0[0:3]
    out[3] = g1[3]
    out[4:8] = g3[...]


def merge_kernel(own, b1, b2, b3, after, *outs):
    for r in range(4):
        total = own[r]
        for other in (b1, b2, b3):
            total = total + other[r].astype(F32)
        outs[r][...] = total.astype(outs[r].dtype)


def halves_kernel(g0, g1, g2, got, out):
    groups = (g0, g1, g2)
    up = 1 - 2 * lax.axis_index("core")
    here = 4 * lax.axis_index("zh") + lax.axis_index("zl") + 8
    for n, (group, place) in enumerate(SAME):
        z = lax.rem(here + up * UP[n], 8)
        out[2 * lax.rem(z, 4) + z // 4] = (groups[group][place] + got[TWIN[n]]).astype(BF)


def last_kernel(u, own, f1, f2, f3, gq, gk, gv):
    total = u[0].astype(F32)
    for z in range(1, 8):
        total = total + u[z].astype(F32)
    gq[...] = total.T * FACTOR
    total = own[...] + f1[...].astype(F32) + f2[...].astype(F32) + f3[...].astype(F32)
    gk[...] = total[0:T] * FACTOR
    gv[...] = total[T:]


SWAP = [(0, 1), (1, 0)]


def swap_cores(x):
    return lax.ppermute(x, "core", SWAP)


def send_z(x, s):
    index = lambda z, c: (z % 4) * 4 + c * 2 + z // 4
    pairs = [
        (index(z, c), index((z + (s if c == 0 else -s)) % 8, c)) for z in range(8) for c in range(2)
    ]
    return lax.ppermute(x, ("zl", "core", "zh"), pairs)


def exchange_z(x):
    return lax.all_to_all(x, ("zl", "zh"), 0, 0, tiled=True)


def send_plane(x, s, core_on_x):
    pairs = []
    for y in range(4):
        for c in range(2):
            for i in range(4):
                to_y, to_x = (y, (i + s) % 4) if c == core_on_x else ((y + s) % 4, i)
                pairs.append(((y * 2 + c) * 4 + i, (to_y * 2 + c) * 4 + to_x))
    return lax.ppermute(x, ("y", "core", "x"), pairs)


def local(queries, keys, values, outputs, out_grad, lse):
    qp, kv = call(
        pack_kernel,
        "pack",
        (sds((QP, W), BF), sds((2 * T, W), BF)),
        (queries, out_grad, outputs, lse.reshape(1, W), keys, values),
        spaces=[ANY] * 6,
        scratch=(
            pltpu.VMEM((W, W), BF),
            pltpu.VMEM((W, W), BF),
            pltpu.VMEM((W, W), BF),
            pltpu.VMEM((1, W), F32),
            pltpu.SemaphoreType.DMA((6,)),
        ),
        vmem=60,
    )
    ks = [send_plane(kv, r, 0) for r in (1, 2, 3)]
    (chip,) = call(pair_kernel, "chip", (sds((2, QP, W), BF),), (qp, swap_cores(qp)), CHIP_COST)
    (kv0,) = call(join_kernel, "join", (sds((4, 2 * T, W), BF),), (kv, *ks), JOIN_COST)
    kv1, kv3 = (send_plane(kv0, s, 1) for s in (1, 3))
    q1, q2 = send_z(chip, 1), send_z(chip, 2)
    (q2_own,) = call(first_kernel, "first", (sds((1, QP, W), BF),), (q2,), FIRST_COST)
    q3, q4 = send_z(q2, 1), send_z(q2_own, 2)
    (part0,), acc = tiles("tiles0e", {0: chip, 3: q1, 4: q2}, ((kv0, (4,), F32, None),), {})
    (mine,) = call(
        gather_kernel,
        "gather",
        (sds((7, QP, W), BF),),
        (q1, q2, q3, q4, kv1, kv3, part0),
        spaces=[VM] * 4 + [ANY] * 3,
    )
    (kv0_late,) = call(
        after_kernel, "late", (sds((4, 2 * T, W), BF),), (kv0, mine), spaces=[VM, ANY]
    )
    kv2 = send_plane(kv0_late, 2, 1)

    sib = swap_cores(mine)
    (part1, part3), acc = tiles(
        "tiles13a",
        {0: chip, 1: mine},
        ((kv1, (0, 1), F32, None), (kv3, (0, 1), F32, None)),
        acc,
    )
    qs = {0: chip, 1: mine, 2: sib}
    (out1, out3), acc = tiles(
        "tiles13b", qs, ((kv1, (2, 3), BF, part1), (kv3, (2, 3), BF, part3)), acc
    )
    back1, back3 = send_plane(out1, -1, 1), send_plane(out3, -3, 1)
    (out2,), acc = tiles("tiles2", qs, ((kv2, (0, 1, 2, 3), BF, None),), acc)
    back2 = send_plane(out2, -2, 1)
    (part0,), acc = tiles("tiles0c", qs, ((kv0, (1, 3), F32, part0),), acc, (back1,))
    (others,) = call(
        stack_kernel, "others", (sds((8, W, W), F32),), (acc[0], acc[1], acc[3])
    )
    rs = swap_cores(others)
    (out0,), acc = tiles("tiles0", qs, ((kv0, (2,), F32, part0),), acc, (back3,))

    (halves,) = call(halves_kernel, "halves", (sds((8, W, W), BF),), (acc[0], acc[1], acc[2], rs))
    u = exchange_z(halves)
    part0, *parts = call(
        merge_kernel,
        "merge",
        (sds((2 * T, W), F32),) + (sds((2 * T, W), BF),) * 3,
        (out0, back1, back2, back3, halves),
        spaces=[VM] * 4 + [ANY],
    )
    f = [send_plane(parts[r - 1], -r, 0) for r in (1, 2, 3)]
    return call(
        last_kernel,
        "last",
        (sds((W, W), F32), sds((T, W), F32), sds((T, W), F32)),
        (u, part0, *f),
    )


def solution(mesh):
    fine = Mesh(mesh.devices.reshape(4, 4, 2, 4, 2), ("zl", "y", "core", "x", "zh"))
    qs, ks = ("x", "zh", "zl", "y", "core"), ("zl", "y", "core", "x", "zh")
    return jax.shard_map(
        local,
        mesh=fine,
        in_specs=(P(qs, None), P(ks, None), P(ks, None), P(qs, None), P(qs, None), P(qs)),
        out_specs=(P(qs, None), P(ks, None), P(ks, None)),
        check_vma=False,
    )
```

```python
import math

import jax
import jax.numpy as jnp
from jax import lax
from jax.experimental import pallas as pl
from jax.experimental.pallas import tpu as pltpu
from jax.sharding import Mesh, PartitionSpec as P

W = 128
JOIN_COST = 20_000_000_000
FIRST_COST = 20_000_000_000
CHIP_COST = 20_000_000_000
T = 240
QP = 2 * W + 16
BF, F32 = jnp.bfloat16, jnp.float32
FACTOR = 1.0 / math.sqrt(W)
LOG2E = math.log2(math.e)
NT = (((1,), (1,)), ((), ()))
NN = (((1,), (0,)), ((), ()))
TN = (((0,), (0,)), ((), ()))
VM = pl.BlockSpec(memory_space=pltpu.VMEM)
ANY = pl.BlockSpec(memory_space=pl.ANY)


def dot(a, b, dims):
    return lax.dot_general(a, b, dims, preferred_element_type=F32)


def call(kernel, name, outs, args, flops=0, aliases=None, spaces=None, scratch=(), vmem=40):
    nbytes = sum(math.prod(a.shape) * a.dtype.itemsize for a in list(outs) + list(args))
    return pl.pallas_call(
        kernel,
        name=name,
        out_shape=outs,
        in_specs=spaces or [VM] * len(args),
        out_specs=tuple([VM] * len(outs)),
        input_output_aliases=aliases or {},
        scratch_shapes=list(scratch),
        compiler_params=pltpu.CompilerParams(vmem_limit_bytes=vmem * 2**20),
        cost_estimate=pl.CostEstimate(flops=flops, bytes_accessed=nbytes, transcendentals=0),
    )(*args)


def sds(shape, dtype):
    return jax.ShapeDtypeStruct(shape, dtype)


def pack_kernel(q, g, o, lse, k, v, qp, kv, qbuf, gbuf, obuf, lbuf, sems):
    moves = (
        (g, gbuf),
        (o, obuf),
        (lse, lbuf),
        (q, qbuf),
        (k, kv.at[pl.ds(0, T), :]),
        (v, kv.at[pl.ds(T, T), :]),
    )
    copies = [pltpu.make_async_copy(src, dst, sems.at[n]) for n, (src, dst) in enumerate(moves)]
    for copy in copies:
        copy.start()
    for copy in copies[:3]:
        copy.wait()
    prod = gbuf[...].astype(F32) * obuf[...].astype(F32)
    delta = jnp.sum(prod.T, axis=0, keepdims=True)
    rows = []
    for x in (lbuf[...] * LOG2E, delta):
        for _ in range(3):
            part = x.astype(BF).astype(F32)
            rows.append(part)
            x = x - part
    rows.append(jnp.zeros((10, W), F32))
    stat = jnp.concatenate(rows, axis=0).astype(BF)
    for copy in copies[3:]:
        copy.wait()
    qp[0:W, :] = qbuf[...]
    qp[W : 2 * W, :] = gbuf[...]
    qp[2 * W :, :] = stat


def pair_kernel(q0, q1, out):
    out[0] = q0[...]
    out[1] = q1[...]


def join_kernel(k0, k1, k2, k3, out):
    for n, k in enumerate((k0, k1, k2, k3)):
        out[n] = k[...]


def after_kernel(x, after, out):
    out[...] = x[...]


def first_kernel(q, out):
    out[...] = q[0:1]


def gather_kernel(q1, q2, q3, q4, kv1, kv3, part, out):
    for n, q in enumerate((q1, q2, q3)):
        out[2 * n : 2 * n + 2] = q[...]
    out[6:7] = q4[...]


GROUPS = (
    ((0, 1), (1, 1), (1, 3), (0, 0)),
    ((1, 0), (1, 2), (1, 4), (1, 5)),
    ((1, 6), (2, 1), (2, 3), (2, 5)),
    ((2, 0), (2, 2), (2, 4), (2, 6)),
    ((0, 1), (3, 1), (4, 1), (0, 0)),
)
SAME = ((0, 3), (1, 0), (1, 1), (1, 2), (2, 0), (2, 1), (2, 2), (2, 3))
UP = (0, -1, -2, -3, -4, 1, 2, 3)
TWIN = (0, 4, 5, 6, 7, 1, 2, 3)


def tiles_kernel(ops, jobs, touched, given, refs):
    qrefs, refs = dict(zip(ops, refs)), refs[len(ops) :]
    kvs, refs = refs[: len(jobs)], refs[len(jobs) :]
    accs = dict(zip(given, refs))
    parts = list(refs[len(given) :])
    refs = refs[len(refs) - len(jobs) - len(touched) :]
    outs, sums = refs[: len(jobs)], dict(zip(touched, refs[len(jobs) :]))
    for kv, out, (sets, has_part) in zip(kvs, outs, jobs):
        part = parts.pop(0) if has_part else None
        ks = jnp.concatenate([kv[i, 0:T, :] for i in range(4)], axis=0)
        vs = jnp.concatenate([kv[i, T:, :] for i in range(4)], axis=0)
        gk = gv = None
        for c in sets:
            mem = GROUPS[c]
            q = jnp.concatenate([qrefs[r][i, 0:W, :] for r, i in mem], axis=0)
            g = jnp.concatenate([qrefs[r][i, W : 2 * W, :] for r, i in mem], axis=0)
            stat = jnp.concatenate([qrefs[r][i, 2 * W :, :].astype(F32) for r, i in mem], axis=1)
            l2 = stat[0:1] + stat[1:2] + stat[2:3]
            delta = stat[3:4] + stat[4:5] + stat[5:6]
            p = jnp.exp2(dot(ks, q, NT) * (FACTOR * LOG2E) - l2)
            ds = (p * (dot(vs, g, NT) - delta)).astype(BF)
            dv = dot(p.astype(BF), g, NN)
            dk = dot(ds, q, NN)
            gv = dv if gv is None else gv + dv
            gk = dk if gk is None else gk + dk
            u = dot(ks, ds, TN)
            c = c % 4
            for n in range(4):
                block = u[:, n * W : (n + 1) * W]
                sums[c][n] = accs[c][n] + block if c in accs else block
            accs[c] = sums[c]
        for i in range(4):
            rows = slice(i * T, (i + 1) * T)
            for col, total in ((slice(0, T), gk), (slice(T, 2 * T), gv)):
                block = total[rows]
                if has_part:
                    block = part[i, col, :] + block
                out[i, col, :] = block.astype(out.dtype)


def tiles(name, queries, jobs, acc, after=()):
    touched = sorted({c % 4 for _, sets, _, _ in jobs for c in sets})
    given = [r for r in touched if r in acc]
    outs = tuple(sds((4, 2 * T, W), dtype) for _, _, dtype, _ in jobs)
    outs += (sds((4, W, W), F32),) * len(touched)
    args = tuple(queries.values()) + tuple(job[0] for job in jobs)
    aliases = {len(args) + n: len(jobs) + touched.index(r) for n, r in enumerate(given)}
    args += tuple(acc[r] for r in given)
    for n, job in enumerate(jobs):
        if job[3] is not None:
            if job[2] == F32:
                aliases[len(args)] = n
            args += (job[3],)
    spaces = [VM] * len(args) + [ANY] * len(after)
    args += tuple(after)
    static = [(sets, part is not None) for _, sets, _, part in jobs]

    def kernel(*refs):
        ins = refs[: len(args) - len(after)]
        tiles_kernel(tuple(queries), static, touched, given, ins + refs[len(args) :])

    flops = sum(10 * 960 * 512 * len(sets) * W for sets, _ in static)
    out = call(kernel, name, outs, args, flops, aliases, spaces)
    return out[: len(jobs)], {**acc, **dict(zip(touched, out[len(jobs) :]))}


def stack_kernel(g0, g1, g3, out):
    out[0:3] = g0[0:3]
    out[3] = g1[3]
    out[4:8] = g3[...]


def merge_kernel(own, b1, b2, b3, after, *outs):
    for r in range(4):
        total = own[r]
        for other in (b1, b2, b3):
            total = total + other[r].astype(F32)
        outs[r][...] = total.astype(outs[r].dtype)


def halves_kernel(g0, g1, g2, got, out):
    groups = (g0, g1, g2)
    up = 1 - 2 * lax.axis_index("core")
    here = 4 * lax.axis_index("zh") + lax.axis_index("zl") + 8
    for n, (group, place) in enumerate(SAME):
        z = lax.rem(here + up * UP[n], 8)
        out[2 * lax.rem(z, 4) + z // 4] = (groups[group][place] + got[TWIN[n]]).astype(BF)


def last_kernel(u, own, f1, f2, f3, gq, gk, gv):
    total = u[0].astype(F32)
    for z in range(1, 8):
        total = total + u[z].astype(F32)
    gq[...] = total.T * FACTOR
    total = own[...] + f1[...].astype(F32) + f2[...].astype(F32) + f3[...].astype(F32)
    gk[...] = total[0:T] * FACTOR
    gv[...] = total[T:]


SWAP = [(0, 1), (1, 0)]


def swap_cores(x):
    return lax.ppermute(x, "core", SWAP)


def send_z(x, s):
    index = lambda z, c: (z % 4) * 4 + c * 2 + z // 4
    pairs = [
        (index(z, c), index((z + (s if c == 0 else -s)) % 8, c)) for z in range(8) for c in range(2)
    ]
    return lax.ppermute(x, ("zl", "core", "zh"), pairs)


def exchange_z(x):
    return lax.all_to_all(x, ("zl", "zh"), 0, 0, tiled=True)


def send_plane(x, s, core_on_x):
    pairs = []
    for y in range(4):
        for c in range(2):
            for i in range(4):
                to_y, to_x = (y, (i + s) % 4) if c == core_on_x else ((y + s) % 4, i)
                pairs.append(((y * 2 + c) * 4 + i, (to_y * 2 + c) * 4 + to_x))
    return lax.ppermute(x, ("y", "core", "x"), pairs)


def local(queries, keys, values, outputs, out_grad, lse):
    qp, kv = call(
        pack_kernel,
        "pack",
        (sds((QP, W), BF), sds((2 * T, W), BF)),
        (queries, out_grad, outputs, lse.reshape(1, W), keys, values),
        spaces=[ANY] * 6,
        scratch=(
            pltpu.VMEM((W, W), BF),
            pltpu.VMEM((W, W), BF),
            pltpu.VMEM((W, W), BF),
            pltpu.VMEM((1, W), F32),
            pltpu.SemaphoreType.DMA((6,)),
        ),
        vmem=60,
    )
    ks = [send_plane(kv, r, 0) for r in (1, 2, 3)]
    (chip,) = call(pair_kernel, "chip", (sds((2, QP, W), BF),), (qp, swap_cores(qp)), CHIP_COST)
    (kv0,) = call(join_kernel, "join", (sds((4, 2 * T, W), BF),), (kv, *ks), JOIN_COST)
    kv1, kv3 = (send_plane(kv0, s, 1) for s in (1, 3))
    q1, q2 = send_z(chip, 1), send_z(chip, 2)
    (q2_own,) = call(first_kernel, "first", (sds((1, QP, W), BF),), (q2,), FIRST_COST)
    q3, q4 = send_z(q2, 1), send_z(q2_own, 2)
    (part0,), acc = tiles("tiles0e", {0: chip, 3: q1, 4: q2}, ((kv0, (4,), F32, None),), {})
    (mine,) = call(
        gather_kernel,
        "gather",
        (sds((7, QP, W), BF),),
        (q1, q2, q3, q4, kv1, kv3, part0),
        spaces=[VM] * 4 + [ANY] * 3,
    )
    sib = swap_cores(mine)
    (part1, part3), acc = tiles(
        "tiles13a",
        {0: chip, 1: mine},
        ((kv1, (0, 1), F32, None), (kv3, (0, 1), F32, None)),
        acc,
    )
    (kv0_late,) = call(
        after_kernel, "late", (sds((4, 2 * T, W), BF),), (kv0, part1), spaces=[VM, ANY]
    )
    kv2 = send_plane(kv0_late, 2, 1)
    qs = {0: chip, 1: mine, 2: sib}
    (out1, out3, part0), acc = tiles(
        "tiles130",
        qs,
        ((kv1, (2, 3), BF, part1), (kv3, (2, 3), BF, part3), (kv0, (1, 3), F32, part0)),
        acc,
    )
    back1, back3 = send_plane(out1, -1, 1), send_plane(out3, -3, 1)
    (out2,), acc = tiles("tiles2", qs, ((kv2, (0, 1, 2, 3), BF, None),), acc)
    (others,) = call(stack_kernel, "others", (sds((8, W, W), F32),), (acc[0], acc[1], acc[3]))
    rs, back2 = swap_cores(others), send_plane(out2, -2, 1)
    (out0,), acc = tiles("tiles0", qs, ((kv0, (2,), F32, part0),), acc, (back1, back3))

    (halves,) = call(halves_kernel, "halves", (sds((8, W, W), BF),), (acc[0], acc[1], acc[2], rs))
    u = exchange_z(halves)
    part0, *parts = call(
        merge_kernel,
        "merge",
        (sds((2 * T, W), F32),) + (sds((2 * T, W), BF),) * 3,
        (out0, back1, back2, back3, halves),
        spaces=[VM] * 4 + [ANY],
    )
    f = [send_plane(parts[r - 1], -r, 0) for r in (1, 2, 3)]
    return call(
        last_kernel,
        "last",
        (sds((W, W), F32), sds((T, W), F32), sds((T, W), F32)),
        (u, part0, *f),
    )


def solution(mesh):
    fine = Mesh(mesh.devices.reshape(4, 4, 2, 4, 2), ("zl", "y", "core", "x", "zh"))
    qs, ks = ("x", "zh", "zl", "y", "core"), ("zl", "y", "core", "x", "zh")
    return jax.shard_map(
        local,
        mesh=fine,
        in_specs=(P(qs, None), P(ks, None), P(ks, None), P(qs, None), P(qs, None), P(qs)),
        out_specs=(P(qs, None), P(ks, None), P(ks, None)),
        check_vma=False,
    )
```
